512 devices in a mesh: dp: 4 (over y_hi, core), chan: 8 (over x, y_lo), seq: 16 (over z).
Axes of the slice: x: 4, y: 4 (y_hi: 2, y_lo: 2; y = y_hi * 2 + y_lo), z: 16, core: 2. Of those that a mesh axis runs over, the one named last changes fastest.
Arguments:
- query_input: bfloat16 [4, 2048, 8192], P('dp', 'seq', 'chan'), may hold values from -6 to 6
- key_input: bfloat16 [4, 2048, 8192], P('dp', 'seq', 'chan'), may hold values from -6 to 6
- value_input: bfloat16 [4, 2048, 8192], P('dp', 'seq', 'chan'), may hold values from -6 to 6
- grad_output: bfloat16 [4, 2048, 8192], P('dp', 'seq', 'chan'), may hold values from -6 to 6
- w_embed: float32 [32, 64], replicated, may hold values from -6 to 6
- w_filter: float32 [64, 8192], P(None, ('chan', 'seq')), may hold values from -0.1875 to 0.1875
- decay_rates: float32 [8192], P(('chan', 'seq')), may hold values from 0.1 to 122.88
Outputs:
- d_query: bfloat16 [4, 2048, 8192], P('dp', 'seq', 'chan')
- d_key: bfloat16 [4, 2048, 8192], P('dp', 'seq', 'chan')
- d_value: bfloat16 [4, 2048, 8192], P('dp', 'seq', 'chan')
- grad_filter: float32 [64, 8192], P(None, ('chan', 'seq'))
- grad_rate: float32 [8192], P(('chan', 'seq'))
- grad_embed: float32 [32, 64], replicated
The draws below stay inside these ranges and needn't reach their ends.
All inputs are finite; a program needn't handle non-finite values.
Results may differ from the reference program's by a relative error of at most 0.0058.
Values may be sent and summed in bfloat16 or wider, within the bound.
No kernel may reach another device: no remote copies, remote signals or barrier semaphores. Data moves between devices by JAX's collectives and lax.ppermute only.
A program may use at most 64 MiB of HBM per device.

```python
import math
import jax
import jax.numpy as jnp
from jax import lax

D = 8192
HID = 64
EMB = 32
LENGTH = 2048
BATCH = 4


def shard_levels(key, shape, pieces, least, high):
    factor_of = 1.0
    for dim, parts in pieces:
        heights = jax.random.uniform(jax.random.fold_in(jax.random.fold_in(key, 6), dim), (parts,), jnp.float32, least / len(pieces), high / len(pieces))
        factor_of = factor_of * jnp.repeat(jnp.exp(heights), shape[dim] // parts).reshape((-1,) + (1,) * (len(shape) - 1 - dim))
    return factor_of


def bell_draw(key, shape, spread, reach, shards=(), held_as=jnp.bfloat16):
    gain = shard_levels(key, shape, shards, -0.22, 0.18) if shards else 1.0
    result = jax.random.normal(key, shape, jnp.float32) * spread * gain
    return jnp.minimum(jnp.maximum(result, -reach), reach).astype(held_as)


def setup_inputs(seed: int = 0) -> dict:
    arg_keys = jax.random.split(jax.random.key(seed), 8)
    return {
        "query_input": bell_draw(arg_keys[0], (BATCH, LENGTH, D), 1.0, 6.0, ((0, 4), (1, 16), (2, 8))),
        "key_input": bell_draw(arg_keys[1], (BATCH, LENGTH, D), 1.0, 6.0, ((0, 4), (1, 16), (2, 8))),
        "value_input": bell_draw(arg_keys[2], (BATCH, LENGTH, D), 1.0, 6.0, ((0, 4), (1, 16), (2, 8))),
        "grad_output": bell_draw(arg_keys[3], (BATCH, LENGTH, D), 1.0, 6.0, ((0, 4), (1, 16), (2, 8))),
        "w_embed": bell_draw(arg_keys[4], (EMB, HID), 1.0, 6.0, (), jnp.float32),
        "w_filter": bell_draw(arg_keys[5], (HID, D), (16 * HID) ** -0.5, 0.1875, ((1, 128),), jnp.float32),
        "decay_rates": jnp.clip(jnp.exp(math.log(122.88) - 7.1137933 * jax.random.uniform(arg_keys[6], (D,), jnp.float32) ** shard_levels(arg_keys[6], (D,), ((0, 128),), -0.2, 0.2)), 0.1, 122.88),
    }


def embed_features(positions, count, length):
    bands = jnp.arange(count // 2, dtype=jnp.float32) + 0.5
    phase = positions[None, :] * bands[:, None] * (2.0 * math.pi / length)
    return jnp.concatenate([jnp.sin(phase), jnp.cos(phase)], axis=0)

def reference(query_input, key_input, value_input, grad_output, w_embed, w_filter, decay_rates):
    batch_count, length, width_total = query_input.shape
    fft_size = 2 * length
    positions = jnp.arange(length, dtype=jnp.float32)
    features = embed_features(positions, w_embed.shape[0], length)
    pre_act = jnp.dot(features.T, w_embed, precision=lax.Precision.HIGHEST)
    hidden = jnp.sin(pre_act)
    block_size = min(256, width_total)
    block_count = width_total // block_size
    loss_scale = 1.0 / math.sqrt(batch_count * length)
    time_scale = 1.0 / math.sqrt(length)

    def one_block(offset):

        def pick(array):
            return lax.dynamic_slice_in_dim(array, offset, block_size, 2).astype(jnp.float32)
        queries = pick(query_input)
        keys_full = pick(key_input)
        values_full = pick(value_input)
        grads_full = pick(grad_output)
        product = (keys_full * values_full).astype(jnp.bfloat16)
        upstream = (grads_full * queries).astype(jnp.bfloat16)
        product, upstream = lax.optimization_barrier((product, upstream))
        product = product.astype(jnp.float32)
        upstream = upstream.astype(jnp.float32)
        filter_block = lax.dynamic_slice_in_dim(w_filter, offset, block_size, 1)
        rate_block = lax.dynamic_slice_in_dim(decay_rates, offset, block_size, 0)
        window = jnp.exp(-rate_block[None, :] * positions[:, None] / length)
        filter_taps = jnp.dot(hidden, filter_block, precision=lax.Precision.HIGHEST) * window
        filter_spec = jnp.fft.rfft(filter_taps, n=fft_size, axis=0)
        input_spec = jnp.fft.rfft(product, n=fft_size, axis=1)
        grad_spec = jnp.fft.rfft(upstream, n=fft_size, axis=1)
        conv_out = jnp.fft.irfft(filter_spec[None] * input_spec, n=fft_size, axis=1)[:, :length]
        conv_grad = jnp.fft.irfft(jnp.conj(filter_spec)[None] * grad_spec, n=fft_size, axis=1)[:, :length]
        correlation = jnp.fft.irfft(jnp.conj(input_spec) * grad_spec, n=fft_size, axis=1)[:, :length]
        correlation = lax.optimization_barrier(jnp.sum(correlation, axis=0)) * loss_scale
        conv_out = lax.optimization_barrier(conv_out.astype(jnp.bfloat16)).astype(jnp.float32)
        conv_grad = lax.optimization_barrier(conv_grad.astype(jnp.bfloat16)).astype(jnp.float32)
        d_query = (grads_full * conv_out).astype(jnp.bfloat16)
        d_key = (conv_grad * values_full).astype(jnp.bfloat16)
        d_value = (conv_grad * keys_full).astype(jnp.bfloat16)
        weighted = correlation * window
        grad_filter = jnp.dot(hidden.T, weighted, precision=lax.Precision.HIGHEST) * time_scale
        grad_rate = -lax.optimization_barrier(jnp.sum(positions[:, None] / length * filter_taps * correlation, axis=0)) * time_scale
        hidden_grad = jnp.dot(weighted, filter_block.T, precision=lax.Precision.HIGHEST)
        return (d_query, d_key, d_value, grad_filter, grad_rate, hidden_grad)
    offsets = (jnp.arange(block_count) * block_size).astype(jnp.int32)
    d_query, d_key, d_value, grad_filter, grad_rate, hidden_grad = lax.map(one_block, offsets)

    def assemble(stacked):
        return jnp.transpose(stacked, (1, 2, 0, 3)).reshape(batch_count, length, width_total)
    grad_filter = jnp.transpose(grad_filter, (1, 0, 2)).reshape(w_filter.shape[0], width_total)
    grad_rate = grad_rate.reshape(width_total)
    hidden_sum = lax.optimization_barrier(jnp.sum(hidden_grad, axis=0))
    grad_embed = jnp.dot(features, hidden_sum * jnp.cos(pre_act), precision=lax.Precision.HIGHEST) * time_scale
    return (assemble(d_query), assemble(d_key), assemble(d_value), grad_filter, grad_rate, grad_embed)
```

```python
import math

import jax
import jax.numpy as jnp
import numpy as np
from jax import lax
from jax.experimental import pallas as pl
from jax.experimental.pallas import tpu as pltpu
from jax.sharding import PartitionSpec as P

BLOCKS = 16
INNER = 128
GROUP = 64
HALF = 17
LENGTH = BLOCKS * INNER
PERIOD = 2 * LENGTH
VMEM = pl.BlockSpec(memory_space=pltpu.VMEM)
PARAMS = pltpu.CompilerParams(vmem_limit_bytes=40 * 1024 * 1024)


def split_table(table):
    high = table.astype(jnp.bfloat16)
    low = (table - high.astype(np.float64)).astype(jnp.bfloat16)
    return np.stack([high, low])


def tables():
    inner = np.arange(INNER)
    angle = 2.0 * math.pi * (np.outer(inner, inner) % INNER) / INNER
    cos, sin = np.cos(angle), np.sin(angle)
    forward = np.block([[cos, -sin], [sin, cos]])
    inverse = np.block([[cos, sin], [-sin, cos]])
    turn = 2.0 * math.pi * np.outer(np.arange(HALF), inner) / PERIOD
    weight = np.full((HALF, 1), 2.0 / PERIOD)
    weight[0] = weight[-1] = 1.0 / PERIOD
    twist = np.stack([np.cos(turn), np.sin(turn)], axis=1).astype(np.float32)
    untwist = np.stack([np.cos(turn) * weight, np.sin(turn) * weight], axis=1).astype(np.float32)
    return split_table(forward), split_table(inverse), twist, untwist


def embed_features(count):
    bands = np.arange(count // 2) + 0.5
    phase = np.arange(LENGTH)[None, :] * bands[:, None] * (2.0 * math.pi / LENGTH)
    return np.concatenate([np.sin(phase), np.cos(phase)], axis=0).astype(np.float32)


def weighted_sum(terms):
    total = None
    for value, factor in terms:
        if abs(factor) < 1e-9:
            continue
        if abs(factor - 1.0) < 1e-9:
            total = value if total is None else total + value
        elif abs(factor + 1.0) < 1e-9:
            total = -value if total is None else total - value
        else:
            part = value * np.float32(factor)
            total = part if total is None else total + part
    return total


def odd_bins(x):
    size = len(x)
    half = size // 2
    if size == 2:
        return {1: (x[0], -x[1])}
    minus = {n: x[n] - x[size - n] for n in range(1, half)}
    plus = {n: x[n] + x[size - n] for n in range(1, half)}
    minus[0] = x[0]
    plus[half] = x[half]
    out = {}
    for k in range(1, half, 2):
        cos = lambda n: math.cos(math.pi * k * n / size)
        sin = lambda n: math.sin(math.pi * k * n / size)
        cos_even = weighted_sum([(minus[n], cos(n)) for n in range(0, half, 2)])
        cos_odd = weighted_sum([(minus[n], cos(n)) for n in range(1, half, 2)])
        sin_even = weighted_sum([(plus[n], sin(n)) for n in range(2, half + 1, 2)])
        sin_odd = weighted_sum([(plus[n], sin(n)) for n in range(1, half, 2)])
        out[k] = (cos_even + cos_odd, -(sin_even + sin_odd))
        out[size - k] = (cos_even - cos_odd, sin_even - sin_odd)
    return out


def real_bins(x):
    size = len(x)
    half = size // 2
    if size == 2:
        return {0: (x[0] + x[1], None), 1: (x[0] - x[1], None)}
    out = {2 * k: v for k, v in real_bins([x[n] + x[n + half] for n in range(half)]).items()}
    out.update(odd_bins([x[n] - x[n + half] for n in range(half)]))
    return out


def outer_bins(x):
    out = {2 * k: v for k, v in real_bins(x).items()}
    out.update(odd_bins(x))
    return out


def odd_times(bins, size):
    half = size // 2
    if size == 2:
        return [bins[1][0], -bins[1][1]]
    ks = range(1, half, 2)
    real_plus = {k: bins[k][0] + bins[size - k][0] for k in ks}
    real_minus = {k: bins[k][0] - bins[size - k][0] for k in ks}
    imag_plus = {k: bins[k][1] + bins[size - k][1] for k in ks}
    imag_minus = {k: bins[k][1] - bins[size - k][1] for k in ks}
    out = [None] * size
    for n in range(half + 1):
        reals, imags = (real_minus, imag_plus) if n % 2 else (real_plus, imag_minus)
        cos = weighted_sum([(reals[k], math.cos(math.pi * k * n / size)) for k in ks])
        sin = weighted_sum([(imags[k], math.sin(math.pi * k * n / size)) for k in ks])
        if n == 0:
            out[0] = cos
        elif n == half:
            out[half] = -sin
        else:
            out[n] = cos - sin
            out[size - n] = -(cos + sin)
    return out


def real_times(bins, size):
    if size == 2:
        return [bins[0][0] + bins[1][0], bins[0][0] - bins[1][0]]
    half = size // 2
    even = real_times({k // 2: v for k, v in bins.items() if k % 2 == 0}, half)
    odd = odd_times({k: v for k, v in bins.items() if k % 2}, half)
    return [even[n] + odd[n] for n in range(half)] + [even[n] - odd[n] for n in range(half)]


def outer_times(bins, size):
    even = real_times({k // 2: v for k, v in bins.items() if k % 2 == 0}, size)
    odd = odd_times({k: v for k, v in bins.items() if k % 2}, size)
    return [even[n] + odd[n] for n in range(size)]


def precise_dot(values, table_ref):
    high = values.astype(jnp.bfloat16)
    low = (values - high.astype(jnp.float32)).astype(jnp.bfloat16)
    dot = lambda a, b: jnp.dot(a, b, preferred_element_type=jnp.float32)
    return dot(high, table_ref[0]) + (dot(low, table_ref[0]) + dot(high, table_ref[1]))


def forward_outer(load, rows, twist_ref, turned_ref):
    @pl.loop(0, rows // 8)
    def _(step):
        where = pl.ds(pl.multiple_of(step * 8, 8), 8)
        bins = outer_bins([load(n, where) for n in range(BLOCKS)])
        for k in range(HALF):
            real, imag = bins[k]
            cos, sin = twist_ref[k, 0:1, :], twist_ref[k, 1:2, :]
            if k == 0:
                turned_real, turned_imag = real, jnp.zeros_like(real)
            elif imag is None:
                turned_real, turned_imag = real * cos, -real * sin
            else:
                turned_real, turned_imag = real * cos + imag * sin, imag * cos - real * sin
            turned_ref[k, where, :INNER] = turned_real
            turned_ref[k, where, INNER:] = turned_imag


def inverse_outer(back_ref, rows, untwist_ref, store):
    @pl.loop(0, rows // 8)
    def _(step):
        where = pl.ds(pl.multiple_of(step * 8, 8), 8)
        bins = {}
        for k in range(HALF):
            real, imag = back_ref[k, where, :INNER], back_ref[k, where, INNER:]
            cos, sin = untwist_ref[k, 0:1, :], untwist_ref[k, 1:2, :]
            if k in (0, HALF - 1):
                bins[k] = (real * cos - imag * sin, None)
            else:
                bins[k] = (real * cos - imag * sin, real * sin + imag * cos)
        for n, value in enumerate(outer_times(bins, BLOCKS)):
            store(n, where, value)


def pack_kernel(query_ref, key_ref, value_ref, grad_ref, sent_ref):
    for first, second, place in ((key_ref, value_ref, 0), (grad_ref, query_ref, GROUP)):
        for pair in range(BLOCKS // 2):
            lanes = slice(2 * GROUP * pair, 2 * GROUP * (pair + 1))
            both = first[0, :, lanes].astype(jnp.float32) * second[0, :, lanes].astype(jnp.float32)
            both = both.T.astype(jnp.bfloat16)
            sent_ref[2 * pair, place : place + GROUP] = both[:GROUP]
            sent_ref[2 * pair + 1, place : place + GROUP] = both[GROUP:]


def filter_kernel(
    hidden_ref, filter_ref, rate_ref, table_ref, twist_ref, window_ref, taps_ref, spec_ref, turned_ref
):
    positions = lax.broadcasted_iota(jnp.int32, (1, LENGTH), 1).astype(jnp.float32)
    window = jnp.exp(-rate_ref[...] * positions / LENGTH)
    window_ref[...] = window
    taps_ref[...] = window * lax.dot_general(
        filter_ref[...],
        hidden_ref[...],
        (((0,), (0,)), ((), ())),
        precision=lax.Precision.HIGHEST,
        preferred_element_type=jnp.float32,
    )
    forward_outer(
        lambda n, where: taps_ref[where, n * INNER : (n + 1) * INNER], GROUP, twist_ref, turned_ref
    )
    turned = turned_ref[...].reshape(HALF * GROUP, 2 * INNER)
    spec_ref[...] = precise_dot(turned, table_ref).reshape(HALF, GROUP, 2 * INNER)


def conv_kernel(
    got_ref, taps_ref, table_ref, back_table_ref, twist_ref, untwist_ref, out_ref, corr_ref, wide_ref, turned_ref, back_ref
):
    wide_ref[...] = got_ref[...].astype(jnp.float32)
    forward_outer(lambda n, where: wide_ref[n, where, :], 2 * GROUP, twist_ref, turned_ref)
    for first, last in ((0, 4), (4, 8), (8, 12), (12, HALF)):
        count = last - first
        turned = turned_ref[first:last].reshape(count * 2 * GROUP, 2 * INNER)
        spec = precise_dot(turned, table_ref).reshape(count, 2 * GROUP, 2 * INNER)
        in_real, in_imag = spec[:, :GROUP, :INNER], spec[:, :GROUP, INNER:]
        up_real, up_imag = spec[:, GROUP:, :INNER], spec[:, GROUP:, INNER:]
        tap_real, tap_imag = taps_ref[first:last, :, :INNER], taps_ref[first:last, :, INNER:]
        joined = jnp.concatenate(
            [
                jnp.concatenate(
                    [tap_real * in_real - tap_imag * in_imag, tap_real * in_imag + tap_imag * in_real],
                    axis=2,
                ),
                jnp.concatenate(
                    [tap_real * up_real + tap_imag * up_imag, tap_real * up_imag - tap_imag * up_real],
                    axis=2,
                ),
            ],
            axis=1,
        )
        corr_ref[first:last, :, :INNER] = in_real * up_real + in_imag * up_imag
        corr_ref[first:last, :, INNER:] = in_real * up_imag - in_imag * up_real
        back = precise_dot(joined.reshape(count * 2 * GROUP, 2 * INNER), back_table_ref)
        back_ref[first:last] = back.reshape(count, 2 * GROUP, 2 * INNER)

    def store(n, where, value):
        wide_ref[n, where, :] = value

    inverse_outer(back_ref, 2 * GROUP, untwist_ref, store)
    out_ref[...] = wide_ref[...].astype(jnp.bfloat16)


def grads_kernel(
    corr_ref, hidden_ref, slope_ref, features_ref, filter_ref, window_ref, taps_ref, back_table_ref, untwist_ref,
    grads_ref, back_ref, corr_time_ref,
):
    back = precise_dot(corr_ref[...].reshape(HALF * GROUP, 2 * INNER), back_table_ref)
    back_ref[...] = back.reshape(HALF, GROUP, 2 * INNER)
    batch_scale = np.float32(1.0 / math.sqrt(4 * LENGTH))
    time_scale = np.float32(1.0 / math.sqrt(LENGTH))

    def store(n, where, value):
        corr_time_ref[where, n * INNER : (n + 1) * INNER] = value * batch_scale

    inverse_outer(back_ref, GROUP, untwist_ref, store)
    corr = corr_time_ref[...]
    weighted = corr * window_ref[...]
    nt = (((1,), (1,)), ((), ()))
    exact = dict(precision=lax.Precision.HIGHEST, preferred_element_type=jnp.float32)
    grads_ref[:, :GROUP] = lax.dot_general(hidden_ref[...], weighted, nt, **exact) * time_scale
    hidden_grad = jnp.dot(filter_ref[...], weighted, **exact) * slope_ref[...]
    grads_ref[:32, GROUP:] = lax.dot_general(features_ref[...], hidden_grad, nt, **exact) * time_scale
    positions = lax.broadcasted_iota(jnp.int32, (1, LENGTH), 1).astype(jnp.float32)
    rate = positions / LENGTH * taps_ref[...] * corr
    ones = jnp.full((32, LENGTH), -time_scale, jnp.float32)
    grads_ref[32:, GROUP:] = lax.dot_general(ones, rate, nt, **exact)


def apply_kernel(got_ref, key_ref, value_ref, grad_ref, d_query_ref, d_key_ref, d_value_ref):
    for pair in range(BLOCKS // 2):
        lanes = slice(2 * GROUP * pair, 2 * GROUP * (pair + 1))

        def times(place):
            both = [got_ref[2 * pair + i, place : place + GROUP].astype(jnp.float32) for i in (0, 1)]
            return jnp.concatenate(both, axis=0).T

        conv, grad = times(0), times(GROUP)
        d_query_ref[0, :, lanes] = (grad_ref[0, :, lanes].astype(jnp.float32) * conv).astype(jnp.bfloat16)
        d_key_ref[0, :, lanes] = (grad * value_ref[0, :, lanes].astype(jnp.float32)).astype(jnp.bfloat16)
        d_value_ref[0, :, lanes] = (grad * key_ref[0, :, lanes].astype(jnp.float32)).astype(jnp.bfloat16)


def call(kernel, outs, ins, scratch=()):
    return pl.pallas_call(
        kernel,
        out_shape=[jax.ShapeDtypeStruct(shape, dtype) for shape, dtype in outs],
        in_specs=[VMEM] * len(ins),
        out_specs=[VMEM] * len(outs),
        scratch_shapes=[pltpu.VMEM(shape, jnp.float32) for shape in scratch],
        compiler_params=PARAMS,
    )(*ins)


def swapped_sum(value, axis, step):
    size = lax.axis_size(axis)
    return value + lax.ppermute(value, axis, [(i, i ^ step) for i in range(size)])


def per_device(query_input, key_input, value_input, grad_output, w_embed, w_filter, decay_rates):
    f32, bf16 = jnp.float32, jnp.bfloat16
    forward, inverse, twist, untwist = (jnp.asarray(t) for t in tables())
    features = jnp.asarray(embed_features(w_embed.shape[0]))
    spectrum = (HALF, GROUP, 2 * INNER)
    both = (HALF, 2 * GROUP, 2 * INNER)
    moved = (BLOCKS, 2 * GROUP, INNER)
    flat = (GROUP, LENGTH)
    (sent,) = call(
        pack_kernel, [(moved, bf16)], (query_input, key_input, value_input, grad_output)
    )
    got = lax.all_to_all(sent, "seq", split_axis=0, concat_axis=0, tiled=True)
    pre = jnp.einsum("ej,et->jt", w_embed, features, precision=lax.Precision.HIGHEST)
    hidden, slope = jnp.sin(pre), jnp.cos(pre)
    window, taps, taps_spec = call(
        filter_kernel,
        [(flat, f32), (flat, f32), (spectrum, f32)],
        (hidden, w_filter, decay_rates[:, None], forward, twist),
        [spectrum],
    )
    result, corr = call(
        conv_kernel,
        [(moved, bf16), (spectrum, f32)],
        (got, taps_spec, forward, inverse, twist, untwist),
        [moved, both, both],
    )
    back = lax.all_to_all(result, "seq", split_axis=0, concat_axis=0, tiled=True)
    (grads,) = call(
        grads_kernel,
        [((GROUP, 2 * GROUP), f32)],
        (corr, hidden, slope, features, w_filter, window, taps, inverse, untwist),
        [spectrum, flat],
    )
    grads = swapped_sum(swapped_sum(grads, "dp", 1), "dp", 2)
    embed = grads[:32, GROUP:]
    for step in (1, 2, 4):
        embed = swapped_sum(embed, "chan", step)
    d_query, d_key, d_value = call(
        apply_kernel,
        [(query_input.shape, bf16)] * 3,
        (back, key_input, value_input, grad_output),
    )
    embed, _ = lax.optimization_barrier((embed, back))
    everyone = jnp.broadcast_to(embed[None], (BLOCKS,) + embed.shape)
    grad_embed = jnp.sum(
        lax.all_to_all(everyone, "seq", split_axis=0, concat_axis=0, tiled=True), axis=0
    )
    return (d_query, d_key, d_value, grads[:, :GROUP], grads[32, GROUP:], grad_embed)


def solution(mesh):
    wide = P("dp", "seq", "chan")
    split = ("chan", "seq")
    return jax.shard_map(
        per_device,
        mesh=mesh,
        in_specs=(wide, wide, wide, wide, P(), P(None, split), P(split)),
        out_specs=(wide, wide, wide, P(None, split), P(split), P()),
        check_vma=False,
    )
```

```python
import math

import jax
import jax.numpy as jnp
import numpy as np
from jax import lax
from jax.experimental import pallas as pl
from jax.experimental.pallas import tpu as pltpu
from jax.sharding import PartitionSpec as P

BLOCKS = 16
INNER = 128
GROUP = 64
HALF = 17
LENGTH = BLOCKS * INNER
PERIOD = 2 * LENGTH
VMEM = pl.BlockSpec(memory_space=pltpu.VMEM)
HBM = pl.BlockSpec(memory_space=pltpu.HBM)


def split_table(table):
    high = table.astype(jnp.bfloat16)
    low = (table - high.astype(np.float64)).astype(jnp.bfloat16)
    return np.stack([high, low])


def tables():
    inner = np.arange(INNER)
    angle = 2.0 * math.pi * (np.outer(inner, inner) % INNER) / INNER
    cos, sin = np.cos(angle), np.sin(angle)
    forward = np.block([[cos, -sin], [sin, cos]])
    turn = 2.0 * math.pi * np.outer(np.arange(HALF), inner) / PERIOD
    weight = np.full((HALF, 1), 2.0 / PERIOD)
    weight[0] = weight[-1] = 1.0 / PERIOD
    turns = np.zeros((4, 24, INNER), np.float32)
    for i, part in enumerate((np.cos(turn), np.sin(turn), np.cos(turn) * weight, np.sin(turn) * weight)):
        turns[i, :HALF] = part
    return split_table(forward), turns


def embed_features(count):
    bands = np.arange(count // 2) + 0.5
    phase = np.arange(LENGTH)[None, :] * bands[:, None] * (2.0 * math.pi / LENGTH)
    return np.concatenate([np.sin(phase), np.cos(phase)], axis=0).astype(np.float32)


def weighted_sum(terms):
    total = None
    for value, factor in terms:
        if abs(factor) < 1e-9:
            continue
        if abs(factor - 1.0) < 1e-9:
            total = value if total is None else total + value
        elif abs(factor + 1.0) < 1e-9:
            total = -value if total is None else total - value
        else:
            part = value * np.float32(factor)
            total = part if total is None else total + part
    return total


def odd_bins(x):
    size = len(x)
    half = size // 2
    if size == 2:
        return {1: (x[0], -x[1])}
    minus = {n: x[n] - x[size - n] for n in range(1, half)}
    plus = {n: x[n] + x[size - n] for n in range(1, half)}
    minus[0] = x[0]
    plus[half] = x[half]
    out = {}
    for k in range(1, half, 2):
        cos = lambda n: math.cos(math.pi * k * n / size)
        sin = lambda n: math.sin(math.pi * k * n / size)
        cos_even = weighted_sum([(minus[n], cos(n)) for n in range(0, half, 2)])
        cos_odd = weighted_sum([(minus[n], cos(n)) for n in range(1, half, 2)])
        sin_even = weighted_sum([(plus[n], sin(n)) for n in range(2, half + 1, 2)])
        sin_odd = weighted_sum([(plus[n], sin(n)) for n in range(1, half, 2)])
        out[k] = (cos_even + cos_odd, -(sin_even + sin_odd))
        out[size - k] = (cos_even - cos_odd, sin_even - sin_odd)
    return out


def real_bins(x):
    size = len(x)
    half = size // 2
    if size == 2:
        return {0: (x[0] + x[1], None), 1: (x[0] - x[1], None)}
    out = {2 * k: v for k, v in real_bins([x[n] + x[n + half] for n in range(half)]).items()}
    out.update(odd_bins([x[n] - x[n + half] for n in range(half)]))
    return out


def outer_bins(x):
    out = {2 * k: v for k, v in real_bins(x).items()}
    out.update(odd_bins(x))
    return out


def odd_times(bins, size):
    half = size // 2
    if size == 2:
        return [bins[1][0], -bins[1][1]]
    ks = range(1, half, 2)
    real_plus = {k: bins[k][0] + bins[size - k][0] for k in ks}
    real_minus = {k: bins[k][0] - bins[size - k][0] for k in ks}
    imag_plus = {k: bins[k][1] + bins[size - k][1] for k in ks}
    imag_minus = {k: bins[k][1] - bins[size - k][1] for k in ks}
    out = [None] * size
    for n in range(half + 1):
        reals, imags = (real_minus, imag_plus) if n % 2 else (real_plus, imag_minus)
        cos = weighted_sum([(reals[k], math.cos(math.pi * k * n / size)) for k in ks])
        sin = weighted_sum([(imags[k], math.sin(math.pi * k * n / size)) for k in ks])
        if n == 0:
            out[0] = cos
        elif n == half:
            out[half] = -sin
        else:
            out[n] = cos - sin
            out[size - n] = -(cos + sin)
    return out


def real_times(bins, size):
    if size == 2:
        return [bins[0][0] + bins[1][0], bins[0][0] - bins[1][0]]
    half = size // 2
    even = real_times({k // 2: v for k, v in bins.items() if k % 2 == 0}, half)
    odd = odd_times({k: v for k, v in bins.items() if k % 2}, half)
    return [even[n] + odd[n] for n in range(half)] + [even[n] - odd[n] for n in range(half)]


def outer_times(bins, size):
    even = real_times({k // 2: v for k, v in bins.items() if k % 2 == 0}, size)
    odd = odd_times({k: v for k, v in bins.items() if k % 2}, size)
    return [even[n] + odd[n] for n in range(size)]


def split(values):
    high = values.astype(jnp.bfloat16)
    return high, (values - high.astype(jnp.float32)).astype(jnp.bfloat16)


def precise_dot(values, table_ref, side=0):
    high, low = split(values)
    dims = (((1,), (side,)), ((), ()))
    dot = lambda a, b: lax.dot_general(a, b, dims, preferred_element_type=jnp.float32)
    return dot(high, table_ref[0]) + (dot(low, table_ref[0]) + dot(high, table_ref[1]))


def forward_outer(load, rows, turns_ref, turned_ref):
    @pl.loop(0, rows // 8)
    def _(step):
        where = pl.ds(pl.multiple_of(step * 8, 8), 8)
        bins = outer_bins([load(n, where) for n in range(BLOCKS)])
        for k in range(HALF):
            real, imag = bins[k]
            cos, sin = turns_ref[0, k : k + 1, :], turns_ref[1, k : k + 1, :]
            if k == 0:
                turned_real, turned_imag = real, jnp.zeros_like(real)
            elif imag is None:
                turned_real, turned_imag = real * cos, -real * sin
            else:
                turned_real, turned_imag = real * cos + imag * sin, imag * cos - real * sin
            turned_ref[k, where, :INNER] = turned_real
            turned_ref[k, where, INNER:] = turned_imag


def inverse_outer(back_ref, offset, rows, turns_ref, store):
    @pl.loop(0, rows // 8)
    def _(step):
        where = pl.ds(pl.multiple_of(step * 8, 8), 8)
        place = pl.ds(pl.multiple_of(offset + step * 8, 8), 8)
        bins = {}
        for k in range(HALF):
            real, imag = back_ref[k, place, :INNER], back_ref[k, place, INNER:]
            cos, sin = turns_ref[2, k : k + 1, :], turns_ref[3, k : k + 1, :]
            if k in (0, HALF - 1):
                bins[k] = (real * cos - imag * sin, None)
            else:
                bins[k] = (real * cos - imag * sin, real * sin + imag * cos)
        for n, value in enumerate(outer_times(bins, BLOCKS)):
            store(n, where, value)


def pack_kernel(
    query_hbm, key_hbm, value_hbm, grad_hbm, sent_hbm, key_ref, value_ref, grad_ref, query_ref, sent_ref, sems, out_sems
):
    pairs = ((key_hbm, key_ref), (value_hbm, value_ref), (grad_hbm, grad_ref), (query_hbm, query_ref))
    copies = []
    for i, (source, target) in enumerate(pairs):
        for half in range(2):
            rows = pl.ds(half * (INNER // 2), INNER // 2)
            copies.append(pltpu.make_async_copy(source.at[0, rows], target.at[rows], sems.at[2 * i + half]))
            copies[-1].start()
    outs = []
    for part, (first, second) in enumerate(((key_ref, value_ref), (grad_ref, query_ref))):
        place = part * GROUP
        for copy in copies[4 * part : 4 * part + 4]:
            copy.wait()
        for pair in range(BLOCKS // 2):
            lanes = slice(2 * GROUP * pair, 2 * GROUP * (pair + 1))
            both = first[:, lanes].astype(jnp.float32) * second[:, lanes].astype(jnp.float32)
            both = both.T.astype(jnp.bfloat16)
            sent_ref[2 * pair, place : place + GROUP] = both[:GROUP]
            sent_ref[2 * pair + 1, place : place + GROUP] = both[GROUP:]
            if part == 1 and pair % 2 == 1:
                where = pl.ds(2 * (pair - 1), 4)
                outs.append(pltpu.make_async_copy(sent_ref.at[where], sent_hbm.at[where], out_sems.at[pair // 2]))
                outs[-1].start()
    for copy in outs:
        copy.wait()


def decay_window(params_ref):
    positions = lax.broadcasted_iota(jnp.int32, (1, LENGTH), 1).astype(jnp.float32)
    return jnp.exp(-params_ref[:, GROUP : GROUP + 1] * positions / LENGTH)


def filter_kernel(hidden_ref, params_ref, table_ref, turns_ref, spec_ref, taps_ref, turned_ref):
    taps_ref[...] = decay_window(params_ref) * lax.dot_general(
        params_ref[:, :GROUP],
        hidden_ref[...],
        (((0,), (0,)), ((), ())),
        precision=lax.Precision.HIGHEST,
        preferred_element_type=jnp.float32,
    )
    forward_outer(
        lambda n, where: taps_ref[where, n * INNER : (n + 1) * INNER], GROUP, turns_ref, turned_ref
    )
    turned = turned_ref[...].reshape(HALF * GROUP, 2 * INNER)
    spec_ref[...] = precise_dot(turned, table_ref).reshape(HALF, GROUP, 2 * INNER)


def precise(a, b, dims):
    (a_high, a_low), (b_high, b_low) = split(a), split(b)
    dot = lambda x, y: lax.dot_general(x, y, (dims, ((), ())), preferred_element_type=jnp.float32)
    return dot(a_high, b_high) + (dot(a_low, b_high) + dot(a_high, b_low))


def spectra(turned_ref, table_ref, first, last):
    count = last - first
    turned = turned_ref[first:last].reshape(count * 2 * GROUP, 2 * INNER)
    spec = precise_dot(turned, table_ref).reshape(count, 2 * GROUP, 2 * INNER)
    in_real, in_imag = spec[:, :GROUP, :INNER], spec[:, :GROUP, INNER:]
    up_real, up_imag = spec[:, GROUP:, :INNER], spec[:, GROUP:, INNER:]
    corr = pair(in_real * up_real + in_imag * up_imag, in_real * up_imag - in_imag * up_real)
    return in_real, in_imag, up_real, up_imag, corr


def pair(real, imag):
    return jnp.concatenate([real, imag], axis=2)


def forward_both(got_ref, wide_ref, turns_ref, turned_ref):
    wide_ref[...] = got_ref[...].astype(jnp.float32)
    forward_outer(lambda n, where: wide_ref[n, where, :], 2 * GROUP, turns_ref, turned_ref)


def weighted_corr(back_ref, offset, params_ref, turns_ref, corr_time_ref):
    def store(n, where, value):
        corr_time_ref[where, n * INNER : (n + 1) * INNER] = value * np.float32(1.0 / math.sqrt(4 * LENGTH))

    inverse_outer(back_ref, offset, GROUP, turns_ref, store)
    return corr_time_ref[...] * decay_window(params_ref)


PARTS = ((0, 4), (4, 8), (8, 12), (12, HALF))
ALONG = ((1,), (1,))
TIME_SCALE = np.float32(1.0 / math.sqrt(LENGTH))


def embed_kernel(
    got_ref, slope_ref, features_ref, params_ref, table_ref, turns_ref, share_ref, wide_ref, turned_ref, back_ref, corr_time_ref
):
    forward_both(got_ref, wide_ref, turns_ref, turned_ref)
    for first, last in PARTS:
        corr = spectra(turned_ref, table_ref, first, last)[4]
        back = precise_dot(corr.reshape((last - first) * GROUP, 2 * INNER), table_ref, 1)
        back_ref[first:last] = back.reshape(last - first, GROUP, 2 * INNER)
    weighted = weighted_corr(back_ref, 0, params_ref, turns_ref, corr_time_ref)
    hidden_grad = precise(params_ref[:, :GROUP], weighted, ((1,), (0,))) * slope_ref[...]
    embed = precise(features_ref[...], hidden_grad, ALONG) * TIME_SCALE
    embed = jnp.concatenate([embed[:16], embed[16:]], axis=1).astype(jnp.bfloat16)
    share_ref[...] = jnp.broadcast_to(embed[None], share_ref.shape)


def main_kernel(
    got_ref, taps_ref, hidden_ref, params_ref, table_ref, turns_ref, out_ref, grads_ref, wide_ref, turned_ref, back_ref, corr_time_ref
):
    forward_both(got_ref, wide_ref, turns_ref, turned_ref)
    for first, last in PARTS:
        in_real, in_imag, up_real, up_imag, corr = spectra(turned_ref, table_ref, first, last)
        tap_real, tap_imag = taps_ref[first:last, :, :INNER], taps_ref[first:last, :, INNER:]
        conv = pair(tap_real * in_real - tap_imag * in_imag, tap_real * in_imag + tap_imag * in_real)
        grad = pair(tap_real * up_real + tap_imag * up_imag, tap_real * up_imag - tap_imag * up_real)
        joined = jnp.concatenate([conv, grad, corr], axis=1)
        back = precise_dot(joined.reshape((last - first) * 3 * GROUP, 2 * INNER), table_ref, 1)
        back_ref[first:last] = back.reshape(last - first, 3 * GROUP, 2 * INNER)

    def store(n, where, value):
        wide_ref[n, where, :] = value

    inverse_outer(back_ref, 0, 2 * GROUP, turns_ref, store)
    for n in range(BLOCKS):
        out_ref[n, : 2 * GROUP] = wide_ref[n].astype(jnp.bfloat16)
        out_ref[n, 2 * GROUP :] = jnp.zeros((16, INNER), jnp.bfloat16)
    weighted = weighted_corr(back_ref, 2 * GROUP, params_ref, turns_ref, corr_time_ref)
    grads_ref[:, :GROUP] = precise(hidden_ref[...], weighted, ALONG) * TIME_SCALE
    slopes = weighted * precise(params_ref[:, :GROUP], hidden_ref[...], ((0,), (0,)))
    inner = lax.broadcasted_iota(jnp.int32, (1, INNER), 1)
    rate = jnp.zeros((GROUP, INNER), jnp.float32)
    for n in range(BLOCKS):
        positions = (inner + n * INNER).astype(jnp.float32) / LENGTH
        rate += positions * slopes[:, n * INNER : (n + 1) * INNER]
    grads_ref[:, GROUP:] = precise(jnp.full((GROUP, INNER), -1.0, jnp.float32), rate, ALONG) * TIME_SCALE


def insert_kernel(shares_ref, _, out_hbm, total_ref, sems):
    total_ref[...] = jnp.sum(shares_ref[...].astype(jnp.float32), axis=0).astype(jnp.bfloat16)
    copies = []
    for n in range(BLOCKS):
        target = out_hbm.at[n, pl.ds(2 * GROUP, 16)]
        copies.append(pltpu.make_async_copy(total_ref, target, sems.at[n]))
        copies[-1].start()
    for copy in copies:
        copy.wait()


def apply_kernel(got_ref, key_ref, value_ref, grad_ref, d_query_ref, d_key_ref, d_value_ref, embed_ref):
    total = jnp.sum(got_ref[:, 2 * GROUP :, :].astype(jnp.float32), axis=0)
    embed_ref[:16] = total[:, :GROUP]
    embed_ref[16:] = total[:, GROUP:]
    for pair in range(BLOCKS // 2):
        lanes = slice(2 * GROUP * pair, 2 * GROUP * (pair + 1))

        def times(place):
            both = [got_ref[2 * pair + i, place : place + GROUP].astype(jnp.float32) for i in (0, 1)]
            return jnp.concatenate(both, axis=0).T

        conv, grad = times(0), times(GROUP)
        d_query_ref[0, :, lanes] = (grad_ref[0, :, lanes].astype(jnp.float32) * conv).astype(jnp.bfloat16)
        d_key_ref[0, :, lanes] = (grad * value_ref[0, :, lanes].astype(jnp.float32)).astype(jnp.bfloat16)
        d_value_ref[0, :, lanes] = (grad * key_ref[0, :, lanes].astype(jnp.float32)).astype(jnp.bfloat16)


def call(kernel, outs, ins, scratch=(), in_specs=None, out_specs=None, aliases=(), megabytes=8):
    return pl.pallas_call(
        kernel,
        out_shape=[jax.ShapeDtypeStruct(shape, dtype) for shape, dtype in outs],
        in_specs=in_specs or [VMEM] * len(ins),
        out_specs=out_specs or [VMEM] * len(outs),
        scratch_shapes=list(scratch),
        input_output_aliases=dict(aliases),
        compiler_params=pltpu.CompilerParams(vmem_limit_bytes=megabytes * 1024 * 1024),
    )(*ins)


def swapped_sum(value, axis, step):
    size = lax.axis_size(axis)
    return value + lax.ppermute(value, axis, [(i, i ^ step) for i in range(size)])


def per_device(query_input, key_input, value_input, grad_output, w_embed, w_filter, decay_rates):
    f32, bf16 = jnp.float32, jnp.bfloat16
    forward, turns = (jnp.asarray(t) for t in tables())
    features = jnp.asarray(embed_features(w_embed.shape[0]))
    spectrum = (HALF, GROUP, 2 * INNER)
    piece = (INNER, query_input.shape[2])
    moved = (BLOCKS, 2 * GROUP, INNER)
    loaded = (BLOCKS, 2 * GROUP + 16, INNER)
    flat = (GROUP, LENGTH)
    (sent,) = call(
        pack_kernel,
        [(moved, bf16)],
        (query_input, key_input, value_input, grad_output),
        [pltpu.VMEM(piece, bf16)] * 4
        + [pltpu.VMEM(moved, bf16), pltpu.SemaphoreType.DMA((8,)), pltpu.SemaphoreType.DMA((4,))],
        in_specs=[HBM] * 4,
        out_specs=[HBM],
        megabytes=58,
    )
    got = lax.all_to_all(sent, "seq", split_axis=0, concat_axis=0, tiled=True)
    pre = jnp.einsum("ej,et->jt", w_embed, features, precision=lax.Precision.HIGHEST)
    hidden, slope = jnp.sin(pre), jnp.cos(pre)
    params = jnp.concatenate(
        [w_filter, jnp.broadcast_to(decay_rates[:, None], (GROUP, INNER - GROUP))], axis=1
    )
    (taps_spec,) = call(
        filter_kernel,
        [(spectrum, f32)],
        (hidden, params, forward, turns),
        [pltpu.VMEM(flat, f32), pltpu.VMEM(spectrum, f32)],
        megabytes=16,
    )
    plane = ("dp", "chan")
    both = (HALF, 2 * GROUP, 2 * INNER)
    got, taps_spec = lax.optimization_barrier((got, taps_spec))
    (shares,) = call(
        embed_kernel,
        [((lax.axis_size(plane), 16, INNER), bf16)],
        (got, slope, features, params, forward, turns),
        [pltpu.VMEM(moved, f32), pltpu.VMEM(both, f32), pltpu.VMEM(spectrum, f32), pltpu.VMEM(flat, f32)],
        megabytes=24,
    )
    shares = lax.all_to_all(shares, plane, split_axis=0, concat_axis=0, tiled=True)
    result, grads = call(
        main_kernel,
        [(loaded, bf16), ((GROUP, 2 * GROUP), f32)],
        (got, taps_spec, hidden, params, forward, turns),
        [
            pltpu.VMEM(moved, f32),
            pltpu.VMEM(both, f32),
            pltpu.VMEM((HALF, 3 * GROUP, 2 * INNER), f32),
            pltpu.VMEM(flat, f32),
        ],
        megabytes=28,
    )
    (result,) = call(
        insert_kernel,
        [(loaded, bf16)],
        (shares, result),
        [pltpu.VMEM((16, INNER), bf16), pltpu.SemaphoreType.DMA((BLOCKS,))],
        in_specs=[VMEM, HBM],
        out_specs=[HBM],
        aliases=((1, 0),),
        megabytes=58,
    )
    result, grads = lax.optimization_barrier((result, grads))
    back = lax.all_to_all(result, "seq", split_axis=0, concat_axis=0, tiled=True)
    grads = swapped_sum(swapped_sum(grads, "dp", 1), "dp", 2)
    d_query, d_key, d_value, grad_embed = call(
        apply_kernel,
        [(query_input.shape, bf16)] * 3 + [(w_embed.shape, f32)],
        (back, key_input, value_input, grad_output),
        megabytes=12,
    )
    return (d_query, d_key, d_value, grads[:, :GROUP], grads[0, GROUP:], grad_embed)


def solution(mesh):
    wide = P("dp", "seq", "chan")
    split = ("chan", "seq")
    return jax.shard_map(
        per_device,
        mesh=mesh,
        in_specs=(wide, wide, wide, wide, P(), P(None, split), P(split)),
        out_specs=(wide, wide, wide, P(None, split), P(split), P()),
        check_vma=False,
    )
```

```python
import math

import jax
import jax.numpy as jnp
import numpy as np
from jax import lax
from jax.experimental import pallas as pl
from jax.experimental.pallas import tpu as pltpu
from jax.sharding import PartitionSpec as P

BLOCKS = 16
INNER = 128
GROUP = 64
HALF = 17
LENGTH = BLOCKS * INNER
PERIOD = 2 * LENGTH
VMEM = pl.BlockSpec(memory_space=pltpu.VMEM)
HBM = pl.BlockSpec(memory_space=pltpu.HBM)


def split_table(table):
    high = table.astype(jnp.bfloat16)
    low = (table - high.astype(np.float64)).astype(jnp.bfloat16)
    return np.stack([high, low])


def tables():
    inner = np.arange(INNER)
    angle = 2.0 * math.pi * (np.outer(inner, inner) % INNER) / INNER
    cos, sin = np.cos(angle), np.sin(angle)
    forward = np.block([[cos, -sin], [sin, cos]])
    turn = 2.0 * math.pi * np.outer(np.arange(HALF), inner) / PERIOD
    weight = np.full((HALF, 1), 2.0 / PERIOD)
    weight[0] = weight[-1] = 1.0 / PERIOD
    turns = np.zeros((4, 24, INNER), np.float32)
    for i, part in enumerate((np.cos(turn), np.sin(turn), np.cos(turn) * weight, np.sin(turn) * weight)):
        turns[i, :HALF] = part
    return split_table(forward), turns


def embed_features(count):
    bands = np.arange(count // 2) + 0.5
    phase = np.arange(LENGTH)[None, :] * bands[:, None] * (2.0 * math.pi / LENGTH)
    return np.concatenate([np.sin(phase), np.cos(phase)], axis=0).astype(np.float32)


def weighted_sum(terms):
    total = None
    for value, factor in terms:
        if abs(factor) < 1e-9:
            continue
        if abs(factor - 1.0) < 1e-9:
            total = value if total is None else total + value
        elif abs(factor + 1.0) < 1e-9:
            total = -value if total is None else total - value
        else:
            part = value * np.float32(factor)
            total = part if total is None else total + part
    return total


def odd_bins(x):
    size = len(x)
    half = size // 2
    if size == 2:
        return {1: (x[0], -x[1])}
    minus = {n: x[n] - x[size - n] for n in range(1, half)}
    plus = {n: x[n] + x[size - n] for n in range(1, half)}
    minus[0] = x[0]
    plus[half] = x[half]
    out = {}
    for k in range(1, half, 2):
        cos = lambda n: math.cos(math.pi * k * n / size)
        sin = lambda n: math.sin(math.pi * k * n / size)
        cos_even = weighted_sum([(minus[n], cos(n)) for n in range(0, half, 2)])
        cos_odd = weighted_sum([(minus[n], cos(n)) for n in range(1, half, 2)])
        sin_even = weighted_sum([(plus[n], sin(n)) for n in range(2, half + 1, 2)])
        sin_odd = weighted_sum([(plus[n], sin(n)) for n in range(1, half, 2)])
        out[k] = (cos_even + cos_odd, -(sin_even + sin_odd))
        out[size - k] = (cos_even - cos_odd, sin_even - sin_odd)
    return out


def real_bins(x):
    size = len(x)
    half = size // 2
    if size == 2:
        return {0: (x[0] + x[1], None), 1: (x[0] - x[1], None)}
    out = {2 * k: v for k, v in real_bins([x[n] + x[n + half] for n in range(half)]).items()}
    out.update(odd_bins([x[n] - x[n + half] for n in range(half)]))
    return out


def outer_bins(x):
    out = {2 * k: v for k, v in real_bins(x).items()}
    out.update(odd_bins(x))
    return out


def odd_times(bins, size):
    half = size // 2
    if size == 2:
        return [bins[1][0], -bins[1][1]]
    ks = range(1, half, 2)
    real_plus = {k: bins[k][0] + bins[size - k][0] for k in ks}
    real_minus = {k: bins[k][0] - bins[size - k][0] for k in ks}
    imag_plus = {k: bins[k][1] + bins[size - k][1] for k in ks}
    imag_minus = {k: bins[k][1] - bins[size - k][1] for k in ks}
    out = [None] * size
    for n in range(half + 1):
        reals, imags = (real_minus, imag_plus) if n % 2 else (real_plus, imag_minus)
        cos = weighted_sum([(reals[k], math.cos(math.pi * k * n / size)) for k in ks])
        sin = weighted_sum([(imags[k], math.sin(math.pi * k * n / size)) for k in ks])
        if n == 0:
            out[0] = cos
        elif n == half:
            out[half] = -sin
        else:
            out[n] = cos - sin
            out[size - n] = -(cos + sin)
    return out


def real_times(bins, size):
    if size == 2:
        return [bins[0][0] + bins[1][0], bins[0][0] - bins[1][0]]
    half = size // 2
    even = real_times({k // 2: v for k, v in bins.items() if k % 2 == 0}, half)
    odd = odd_times({k: v for k, v in bins.items() if k % 2}, half)
    return [even[n] + odd[n] for n in range(half)] + [even[n] - odd[n] for n in range(half)]


def outer_times(bins, size):
    even = real_times({k // 2: v for k, v in bins.items() if k % 2 == 0}, size)
    odd = odd_times({k: v for k, v in bins.items() if k % 2}, size)
    return [even[n] + odd[n] for n in range(size)]


def split(values):
    high = values.astype(jnp.bfloat16)
    return high, (values - high.astype(jnp.float32)).astype(jnp.bfloat16)


def precise_dot(values, table_ref, side=0, brief=False):
    high, low = split(values)
    dims = (((1,), (side,)), ((), ()))
    dot = lambda a, b: lax.dot_general(a, b, dims, preferred_element_type=jnp.float32)
    rest = dot(high, table_ref[1])
    if not brief:
        rest = dot(low, table_ref[0]) + rest
    return dot(high, table_ref[0]) + rest


def forward_outer(load, rows, turns_ref, turned_ref):
    @pl.loop(0, rows // 8)
    def _(step):
        where = pl.ds(pl.multiple_of(step * 8, 8), 8)
        bins = outer_bins([load(n, where) for n in range(BLOCKS)])
        for k in range(HALF):
            real, imag = bins[k]
            cos, sin = turns_ref[0, k : k + 1, :], turns_ref[1, k : k + 1, :]
            if k == 0:
                turned_real, turned_imag = real, jnp.zeros_like(real)
            elif imag is None:
                turned_real, turned_imag = real * cos, -real * sin
            else:
                turned_real, turned_imag = real * cos + imag * sin, imag * cos - real * sin
            turned_ref[k, where, :INNER] = turned_real
            turned_ref[k, where, INNER:] = turned_imag


def inverse_outer(back_ref, rows, turns_ref, store):
    @pl.loop(0, rows // 8)
    def _(step):
        where = pl.ds(pl.multiple_of(step * 8, 8), 8)
        bins = {}
        for k in range(HALF):
            real, imag = back_ref[k, where, :INNER], back_ref[k, where, INNER:]
            cos, sin = turns_ref[2, k : k + 1, :], turns_ref[3, k : k + 1, :]
            if k in (0, HALF - 1):
                bins[k] = (real * cos - imag * sin, None)
            else:
                bins[k] = (real * cos - imag * sin, real * sin + imag * cos)
        for n, value in enumerate(outer_times(bins, BLOCKS)):
            store(n, where, value)


def pack_kernel(
    query_hbm, key_hbm, value_hbm, grad_hbm, sent_hbm, key_ref, value_ref, grad_ref, query_ref, sent_ref, sems, out_sems
):
    sources = (key_hbm, value_hbm, grad_hbm, query_hbm)
    targets = (key_ref, value_ref, grad_ref, query_ref)
    copies = {}
    for part in range(4):
        lanes = pl.ds(4 * GROUP * part, 4 * GROUP)
        for i in range(4):
            source, target = sources[i].at[0, :, lanes], targets[i].at[:, lanes]
            copies[part, i] = pltpu.make_async_copy(source, target, sems.at[4 * part + i])
            copies[part, i].start()
    outs = []
    for part in range(4):
        for i in range(4):
            copies[part, i].wait()
        for pair in (2 * part, 2 * part + 1):
            lanes = slice(2 * GROUP * pair, 2 * GROUP * (pair + 1))
            for place, first, second in ((0, key_ref, value_ref), (GROUP, grad_ref, query_ref)):
                both = first[:, lanes].astype(jnp.float32) * second[:, lanes].astype(jnp.float32)
                both = both.T.astype(jnp.bfloat16)
                sent_ref[2 * pair, place : place + GROUP] = both[:GROUP]
                sent_ref[2 * pair + 1, place : place + GROUP] = both[GROUP:]
        where = pl.ds(4 * part, 4)
        outs.append(pltpu.make_async_copy(sent_ref.at[where], sent_hbm.at[where], out_sems.at[part]))
        outs[-1].start()
    for copy in outs:
        copy.wait()


def decay_window(params_ref):
    positions = lax.broadcasted_iota(jnp.int32, (1, LENGTH), 1).astype(jnp.float32)
    return jnp.exp(-params_ref[:, GROUP : GROUP + 1] * positions / LENGTH)


def filter_kernel(hidden_ref, params_ref, table_ref, turns_ref, spec_ref, taps_ref, turned_ref):
    taps_ref[...] = decay_window(params_ref) * lax.dot_general(
        params_ref[:, :GROUP],
        hidden_ref[...],
        (((0,), (0,)), ((), ())),
        precision=lax.Precision.HIGHEST,
        preferred_element_type=jnp.float32,
    )
    forward_outer(
        lambda n, where: taps_ref[where, n * INNER : (n + 1) * INNER], GROUP, turns_ref, turned_ref
    )
    turned = turned_ref[...].reshape(HALF * GROUP, 2 * INNER)
    spec_ref[...] = precise_dot(turned, table_ref).reshape(HALF, GROUP, 2 * INNER)


def precise(a, b, dims):
    (a_high, a_low), (b_high, b_low) = split(a), split(b)
    dot = lambda x, y: lax.dot_general(x, y, (dims, ((), ())), preferred_element_type=jnp.float32)
    return dot(a_high, b_high) + (dot(a_low, b_high) + dot(a_high, b_low))


def spectra(turned_ref, table_ref, first, last, brief=False):
    count = last - first
    turned = turned_ref[first:last].reshape(count * 2 * GROUP, 2 * INNER)
    spec = precise_dot(turned, table_ref, brief=brief).reshape(count, 2 * GROUP, 2 * INNER)
    in_real, in_imag = spec[:, :GROUP, :INNER], spec[:, :GROUP, INNER:]
    up_real, up_imag = spec[:, GROUP:, :INNER], spec[:, GROUP:, INNER:]
    corr = pair(in_real * up_real + in_imag * up_imag, in_real * up_imag - in_imag * up_real)
    return in_real, in_imag, up_real, up_imag, corr


def pair(real, imag):
    return jnp.concatenate([real, imag], axis=2)


def forward_both(got_ref, wide_ref, turns_ref, turned_ref):
    wide_ref[...] = got_ref[...].astype(jnp.float32)
    forward_outer(lambda n, where: wide_ref[n, where, :], 2 * GROUP, turns_ref, turned_ref)


def weighted_corr(got_ref, params_ref, table_ref, turns_ref, wide_ref, turned_ref, back_ref, corr_time_ref, brief):
    forward_both(got_ref, wide_ref, turns_ref, turned_ref)
    for first, last in PARTS:
        corr = spectra(turned_ref, table_ref, first, last, brief)[4]
        back = precise_dot(corr.reshape((last - first) * GROUP, 2 * INNER), table_ref, 1, brief)
        back_ref[first:last] = back.reshape(last - first, GROUP, 2 * INNER)

    def store(n, where, value):
        corr_time_ref[where, n * INNER : (n + 1) * INNER] = value * np.float32(1.0 / math.sqrt(4 * LENGTH))

    inverse_outer(back_ref, GROUP, turns_ref, store)
    return corr_time_ref[...] * decay_window(params_ref)


PARTS = ((0, 4), (4, 8), (8, 12), (12, HALF))
ALONG = ((1,), (1,))
TIME_SCALE = np.float32(1.0 / math.sqrt(LENGTH))


def embed_kernel(
    got_ref, slope_ref, features_ref, params_ref, table_ref, turns_ref, share_ref, wide_ref, turned_ref, back_ref, corr_time_ref
):
    weighted = weighted_corr(
        got_ref, params_ref, table_ref, turns_ref, wide_ref, turned_ref, back_ref, corr_time_ref, True
    )
    hidden_grad = precise(params_ref[:, :GROUP], weighted, ((1,), (0,))) * slope_ref[...]
    embed = precise(features_ref[...], hidden_grad, ALONG) * TIME_SCALE
    embed = jnp.concatenate([embed[:16], embed[16:]], axis=1).astype(jnp.bfloat16)
    share_ref[...] = jnp.broadcast_to(embed[None], share_ref.shape)


def conv_kernel(got_ref, taps_ref, table_ref, turns_ref, out_ref, wide_ref, turned_ref, back_ref):
    forward_both(got_ref, wide_ref, turns_ref, turned_ref)
    for first, last in PARTS:
        in_real, in_imag, up_real, up_imag, _ = spectra(turned_ref, table_ref, first, last)
        tap_real, tap_imag = taps_ref[first:last, :, :INNER], taps_ref[first:last, :, INNER:]
        conv = pair(tap_real * in_real - tap_imag * in_imag, tap_real * in_imag + tap_imag * in_real)
        grad = pair(tap_real * up_real + tap_imag * up_imag, tap_real * up_imag - tap_imag * up_real)
        joined = jnp.concatenate([conv, grad], axis=1)
        back = precise_dot(joined.reshape((last - first) * 2 * GROUP, 2 * INNER), table_ref, 1)
        back_ref[first:last] = back.reshape(last - first, 2 * GROUP, 2 * INNER)

    def store(n, where, value):
        wide_ref[n, where, :] = value

    inverse_outer(back_ref, 2 * GROUP, turns_ref, store)
    for n in range(BLOCKS):
        out_ref[n, : 2 * GROUP] = wide_ref[n].astype(jnp.bfloat16)
        out_ref[n, 2 * GROUP :] = jnp.zeros((16, INNER), jnp.bfloat16)


def grads_kernel(
    got_ref, hidden_ref, params_ref, table_ref, turns_ref, grads_ref, wide_ref, turned_ref, back_ref, corr_time_ref
):
    weighted = weighted_corr(
        got_ref, params_ref, table_ref, turns_ref, wide_ref, turned_ref, back_ref, corr_time_ref, False
    )
    grads_ref[:, :GROUP] = precise(hidden_ref[...], weighted, ALONG) * TIME_SCALE
    slopes = weighted * precise(params_ref[:, :GROUP], hidden_ref[...], ((0,), (0,)))
    inner = lax.broadcasted_iota(jnp.int32, (1, INNER), 1)
    rate = jnp.zeros((GROUP, INNER), jnp.float32)
    for n in range(BLOCKS):
        positions = (inner + n * INNER).astype(jnp.float32) / LENGTH
        rate += positions * slopes[:, n * INNER : (n + 1) * INNER]
    grads_ref[:, GROUP:] = precise(jnp.full((GROUP, INNER), -1.0, jnp.float32), rate, ALONG) * TIME_SCALE


def insert_kernel(shares_ref, _, out_hbm, total_ref, sems):
    total_ref[...] = jnp.sum(shares_ref[...].astype(jnp.float32), axis=0).astype(jnp.bfloat16)
    copies = []
    for n in range(BLOCKS):
        target = out_hbm.at[n, pl.ds(2 * GROUP, 16)]
        copies.append(pltpu.make_async_copy(total_ref, target, sems.at[n]))
        copies[-1].start()
    for copy in copies:
        copy.wait()


def apply_kernel(got_ref, key_ref, value_ref, grad_ref, d_query_ref, d_key_ref, d_value_ref, embed_ref):
    total = jnp.sum(got_ref[:, 2 * GROUP :, :].astype(jnp.float32), axis=0)
    embed_ref[:16] = total[:, :GROUP]
    embed_ref[16:] = total[:, GROUP:]
    for pair in range(BLOCKS // 2):
        lanes = slice(2 * GROUP * pair, 2 * GROUP * (pair + 1))

        def times(place):
            both = [got_ref[2 * pair + i, place : place + GROUP].astype(jnp.float32) for i in (0, 1)]
            return jnp.concatenate(both, axis=0).T

        conv, grad = times(0), times(GROUP)
        d_query_ref[0, :, lanes] = (grad_ref[0, :, lanes].astype(jnp.float32) * conv).astype(jnp.bfloat16)
        d_key_ref[0, :, lanes] = (grad * value_ref[0, :, lanes].astype(jnp.float32)).astype(jnp.bfloat16)
        d_value_ref[0, :, lanes] = (grad * key_ref[0, :, lanes].astype(jnp.float32)).astype(jnp.bfloat16)


def call(kernel, outs, ins, scratch=(), in_specs=None, out_specs=None, aliases=(), megabytes=8):
    return pl.pallas_call(
        kernel,
        out_shape=[jax.ShapeDtypeStruct(shape, dtype) for shape, dtype in outs],
        in_specs=in_specs or [VMEM] * len(ins),
        out_specs=out_specs or [VMEM] * len(outs),
        scratch_shapes=list(scratch),
        input_output_aliases=dict(aliases),
        compiler_params=pltpu.CompilerParams(vmem_limit_bytes=megabytes * 1024 * 1024),
    )(*ins)


def swapped_sum(value, axis, step):
    size = lax.axis_size(axis)
    return value + lax.ppermute(value, axis, [(i, i ^ step) for i in range(size)])


def per_device(query_input, key_input, value_input, grad_output, w_embed, w_filter, decay_rates):
    f32, bf16 = jnp.float32, jnp.bfloat16
    forward, turns = (jnp.asarray(t) for t in tables())
    features = jnp.asarray(embed_features(w_embed.shape[0]))
    spectrum = (HALF, GROUP, 2 * INNER)
    piece = (INNER, query_input.shape[2])
    moved = (BLOCKS, 2 * GROUP, INNER)
    loaded = (BLOCKS, 2 * GROUP + 16, INNER)
    flat = (GROUP, LENGTH)
    (sent,) = call(
        pack_kernel,
        [(moved, bf16)],
        (query_input, key_input, value_input, grad_output),
        [pltpu.VMEM(piece, bf16)] * 4
        + [pltpu.VMEM(moved, bf16), pltpu.SemaphoreType.DMA((16,)), pltpu.SemaphoreType.DMA((4,))],
        in_specs=[HBM] * 4,
        out_specs=[HBM],
        megabytes=58,
    )
    got = lax.all_to_all(sent, "seq", split_axis=0, concat_axis=0, tiled=True)
    pre = jnp.einsum("ej,et->jt", w_embed, features, precision=lax.Precision.HIGHEST)
    hidden, slope = jnp.sin(pre), jnp.cos(pre)
    params = jnp.concatenate(
        [w_filter, jnp.broadcast_to(decay_rates[:, None], (GROUP, INNER - GROUP))], axis=1
    )
    (taps_spec,) = call(
        filter_kernel,
        [(spectrum, f32)],
        (hidden, params, forward, turns),
        [pltpu.VMEM(flat, f32), pltpu.VMEM(spectrum, f32)],
        megabytes=16,
    )
    plane = ("dp", "chan")
    both = (HALF, 2 * GROUP, 2 * INNER)
    got, taps_spec = lax.optimization_barrier((got, taps_spec))
    corr_scratch = [pltpu.VMEM(shape, f32) for shape in (moved, both, spectrum, flat)]
    (shares,) = call(
        embed_kernel,
        [((lax.axis_size(plane), 16, INNER), bf16)],
        (got, slope, features, params, forward, turns),
        corr_scratch,
        megabytes=24,
    )
    shares = lax.all_to_all(shares, plane, split_axis=0, concat_axis=0, tiled=True)
    (result,) = call(
        conv_kernel,
        [(loaded, bf16)],
        (got, taps_spec, forward, turns),
        [pltpu.VMEM(moved, f32), pltpu.VMEM(both, f32), pltpu.VMEM(both, f32)],
        megabytes=24,
    )
    (result,) = call(
        insert_kernel,
        [(loaded, bf16)],
        (shares, result),
        [pltpu.VMEM((16, INNER), bf16), pltpu.SemaphoreType.DMA((BLOCKS,))],
        in_specs=[VMEM, HBM],
        out_specs=[HBM],
        aliases=((1, 0),),
        megabytes=4,
    )
    result, got = lax.optimization_barrier((result, got))
    back = lax.all_to_all(result, "seq", split_axis=0, concat_axis=0, tiled=True)
    (grads,) = call(
        grads_kernel,
        [((GROUP, 2 * GROUP), f32)],
        (got, hidden, params, forward, turns),
        corr_scratch,
        megabytes=24,
    )
    grads = swapped_sum(swapped_sum(grads, "dp", 1), "dp", 2)
    d_query, d_key, d_value, grad_embed = call(
        apply_kernel,
        [(query_input.shape, bf16)] * 3 + [(w_embed.shape, f32)],
        (back, key_input, value_input, grad_output),
        megabytes=12,
    )
    return (d_query, d_key, d_value, grads[:, :GROUP], grads[0, GROUP:], grad_embed)


def solution(mesh):
    wide = P("dp", "seq", "chan")
    split = ("chan", "seq")
    return jax.shard_map(
        per_device,
        mesh=mesh,
        in_specs=(wide, wide, wide, wide, P(), P(None, split), P(split)),
        out_specs=(wide, wide, wide, P(None, split), P(split), P()),
        check_vma=False,
    )
```

```python
import math

import jax
import jax.numpy as jnp
import numpy as np
from jax import lax
from jax.experimental import pallas as pl
from jax.experimental.pallas import tpu as pltpu
from jax.sharding import PartitionSpec as P

BLOCKS = 16
INNER = 128
GROUP = 64
HALF = 17
LENGTH = BLOCKS * INNER
PERIOD = 2 * LENGTH
VMEM = pl.BlockSpec(memory_space=pltpu.VMEM)
HBM = pl.BlockSpec(memory_space=pltpu.HBM)


def split_table(table):
    high = table.astype(jnp.bfloat16)
    low = (table - high.astype(np.float64)).astype(jnp.bfloat16)
    return np.stack([high, low])


def tables():
    inner = np.arange(INNER)
    angle = 2.0 * math.pi * (np.outer(inner, inner) % INNER) / INNER
    cos, sin = np.cos(angle), np.sin(angle)
    forward = np.block([[cos, -sin], [sin, cos]])
    turn = 2.0 * math.pi * np.outer(np.arange(HALF), inner) / PERIOD
    weight = np.full((HALF, 1), 2.0 / PERIOD)
    weight[0] = weight[-1] = 1.0 / PERIOD
    turns = np.zeros((4, 24, INNER), np.float32)
    for i, part in enumerate((np.cos(turn), np.sin(turn), np.cos(turn) * weight, np.sin(turn) * weight)):
        turns[i, :HALF] = part
    return split_table(forward), turns


def embed_features(count):
    bands = np.arange(count // 2) + 0.5
    phase = np.arange(LENGTH)[None, :] * bands[:, None] * (2.0 * math.pi / LENGTH)
    return np.concatenate([np.sin(phase), np.cos(phase)], axis=0).astype(np.float32)


def weighted_sum(terms):
    total = None
    for value, factor in terms:
        if abs(factor) < 1e-9:
            continue
        if abs(factor - 1.0) < 1e-9:
            total = value if total is None else total + value
        elif abs(factor + 1.0) < 1e-9:
            total = -value if total is None else total - value
        else:
            part = value * np.float32(factor)
            total = part if total is None else total + part
    return total


def odd_bins(x):
    size = len(x)
    half = size // 2
    if size == 2:
        return {1: (x[0], -x[1])}
    minus = {n: x[n] - x[size - n] for n in range(1, half)}
    plus = {n: x[n] + x[size - n] for n in range(1, half)}
    minus[0] = x[0]
    plus[half] = x[half]
    out = {}
    for k in range(1, half, 2):
        cos = lambda n: math.cos(math.pi * k * n / size)
        sin = lambda n: math.sin(math.pi * k * n / size)
        cos_even = weighted_sum([(minus[n], cos(n)) for n in range(0, half, 2)])
        cos_odd = weighted_sum([(minus[n], cos(n)) for n in range(1, half, 2)])
        sin_even = weighted_sum([(plus[n], sin(n)) for n in range(2, half + 1, 2)])
        sin_odd = weighted_sum([(plus[n], sin(n)) for n in range(1, half, 2)])
        out[k] = (cos_even + cos_odd, -(sin_even + sin_odd))
        out[size - k] = (cos_even - cos_odd, sin_even - sin_odd)
    return out


def real_bins(x):
    size = len(x)
    half = size // 2
    if size == 2:
        return {0: (x[0] + x[1], None), 1: (x[0] - x[1], None)}
    out = {2 * k: v for k, v in real_bins([x[n] + x[n + half] for n in range(half)]).items()}
    out.update(odd_bins([x[n] - x[n + half] for n in range(half)]))
    return out


def outer_bins(x):
    out = {2 * k: v for k, v in real_bins(x).items()}
    out.update(odd_bins(x))
    return out


def odd_times(bins, size):
    half = size // 2
    if size == 2:
        return [bins[1][0], -bins[1][1]]
    ks = range(1, half, 2)
    real_plus = {k: bins[k][0] + bins[size - k][0] for k in ks}
    real_minus = {k: bins[k][0] - bins[size - k][0] for k in ks}
    imag_plus = {k: bins[k][1] + bins[size - k][1] for k in ks}
    imag_minus = {k: bins[k][1] - bins[size - k][1] for k in ks}
    out = [None] * size
    for n in range(half + 1):
        reals, imags = (real_minus, imag_plus) if n % 2 else (real_plus, imag_minus)
        cos = weighted_sum([(reals[k], math.cos(math.pi * k * n / size)) for k in ks])
        sin = weighted_sum([(imags[k], math.sin(math.pi * k * n / size)) for k in ks])
        if n == 0:
            out[0] = cos
        elif n == half:
            out[half] = -sin
        else:
            out[n] = cos - sin
            out[size - n] = -(cos + sin)
    return out


def real_times(bins, size):
    if size == 2:
        return [bins[0][0] + bins[1][0], bins[0][0] - bins[1][0]]
    half = size // 2
    even = real_times({k // 2: v for k, v in bins.items() if k % 2 == 0}, half)
    odd = odd_times({k: v for k, v in bins.items() if k % 2}, half)
    return [even[n] + odd[n] for n in range(half)] + [even[n] - odd[n] for n in range(half)]


def outer_times(bins, size):
    even = real_times({k // 2: v for k, v in bins.items() if k % 2 == 0}, size)
    odd = odd_times({k: v for k, v in bins.items() if k % 2}, size)
    return [even[n] + odd[n] for n in range(size)]


def split(values):
    high = values.astype(jnp.bfloat16)
    return high, (values - high.astype(jnp.float32)).astype(jnp.bfloat16)


def precise_dot(values, table_ref, side=0, brief=False):
    high, low = split(values)
    dims = (((1,), (side,)), ((), ()))
    dot = lambda a, b: lax.dot_general(a, b, dims, preferred_element_type=jnp.float32)
    rest = dot(high, table_ref[1])
    if not brief:
        rest = dot(low, table_ref[0]) + rest
    return dot(high, table_ref[0]) + rest


def forward_outer(load, rows, turns_ref, turned_ref):
    @pl.loop(0, rows // 8, unroll=2)
    def _(step):
        where = pl.ds(pl.multiple_of(step * 8, 8), 8)
        bins = outer_bins([load(n, where) for n in range(BLOCKS)])
        for k in range(HALF):
            real, imag = bins[k]
            cos, sin = turns_ref[0, k : k + 1, :], turns_ref[1, k : k + 1, :]
            if k == 0:
                turned_real, turned_imag = real, jnp.zeros_like(real)
            elif imag is None:
                turned_real, turned_imag = real * cos, -real * sin
            else:
                turned_real, turned_imag = real * cos + imag * sin, imag * cos - real * sin
            turned_ref[k, where, :INNER] = turned_real
            turned_ref[k, where, INNER:] = turned_imag


def inverse_outer(back_ref, rows, turns_ref, store):
    @pl.loop(0, rows // 8, unroll=2)
    def _(step):
        where = pl.ds(pl.multiple_of(step * 8, 8), 8)
        bins = {}
        for k in range(HALF):
            real, imag = back_ref[k, where, :INNER], back_ref[k, where, INNER:]
            cos, sin = turns_ref[2, k : k + 1, :], turns_ref[3, k : k + 1, :]
            if k in (0, HALF - 1):
                bins[k] = (real * cos - imag * sin, None)
            else:
                bins[k] = (real * cos - imag * sin, real * sin + imag * cos)
        for n, value in enumerate(outer_times(bins, BLOCKS)):
            store(n, where, value)


def pack_kernel(
    query_hbm, key_hbm, value_hbm, grad_hbm, sent_hbm, key_ref, value_ref, grad_ref, query_ref, sent_ref, sems, out_sems
):
    sources = (key_hbm, value_hbm, grad_hbm, query_hbm)
    targets = (key_ref, value_ref, grad_ref, query_ref)
    copies = {}
    for part in range(4):
        lanes = pl.ds(4 * GROUP * part, 4 * GROUP)
        for i in range(4):
            source, target = sources[i].at[0, :, lanes], targets[i].at[:, lanes]
            copies[part, i] = pltpu.make_async_copy(source, target, sems.at[4 * part + i])
            copies[part, i].start()
    outs = []
    for part in range(4):
        for i in range(4):
            copies[part, i].wait()
        for pair in (2 * part, 2 * part + 1):
            lanes = slice(2 * GROUP * pair, 2 * GROUP * (pair + 1))
            for place, first, second in ((0, key_ref, value_ref), (GROUP, grad_ref, query_ref)):
                both = first[:, lanes].astype(jnp.float32) * second[:, lanes].astype(jnp.float32)
                both = both.T.astype(jnp.bfloat16)
                sent_ref[2 * pair, place : place + GROUP] = both[:GROUP]
                sent_ref[2 * pair + 1, place : place + GROUP] = both[GROUP:]
        where = pl.ds(4 * part, 4)
        outs.append(pltpu.make_async_copy(sent_ref.at[where], sent_hbm.at[where], out_sems.at[part]))
        outs[-1].start()
    for copy in outs:
        copy.wait()


def decay_window(params_ref):
    positions = lax.broadcasted_iota(jnp.int32, (1, LENGTH), 1).astype(jnp.float32)
    return jnp.exp(-params_ref[:, GROUP : GROUP + 1] * positions / LENGTH)


def filter_kernel(hidden_ref, params_ref, table_ref, turns_ref, spec_ref, taps_ref, turned_ref):
    taps_ref[...] = decay_window(params_ref) * lax.dot_general(
        params_ref[:, :GROUP],
        hidden_ref[...],
        (((0,), (0,)), ((), ())),
        precision=lax.Precision.HIGHEST,
        preferred_element_type=jnp.float32,
    )
    forward_outer(
        lambda n, where: taps_ref[where, n * INNER : (n + 1) * INNER], GROUP, turns_ref, turned_ref
    )
    turned = turned_ref[...].reshape(HALF * GROUP, 2 * INNER)
    spec_ref[...] = precise_dot(turned, table_ref).reshape(HALF, GROUP, 2 * INNER)


def precise(a, b, dims):
    (a_high, a_low), (b_high, b_low) = split(a), split(b)
    dot = lambda x, y: lax.dot_general(x, y, (dims, ((), ())), preferred_element_type=jnp.float32)
    return dot(a_high, b_high) + (dot(a_low, b_high) + dot(a_high, b_low))


def spectra(turned_ref, table_ref, first, last, brief=False):
    count = last - first
    turned = turned_ref[first:last].reshape(count * 2 * GROUP, 2 * INNER)
    spec = precise_dot(turned, table_ref, brief=brief).reshape(count, 2 * GROUP, 2 * INNER)
    in_real, in_imag = spec[:, :GROUP, :INNER], spec[:, :GROUP, INNER:]
    up_real, up_imag = spec[:, GROUP:, :INNER], spec[:, GROUP:, INNER:]
    corr = pair(in_real * up_real + in_imag * up_imag, in_real * up_imag - in_imag * up_real)
    return in_real, in_imag, up_real, up_imag, corr


def pair(real, imag):
    return jnp.concatenate([real, imag], axis=2)


def forward_both(got_ref, wide_ref, turns_ref, turned_ref):
    wide_ref[...] = got_ref[...].astype(jnp.float32)
    forward_outer(lambda n, where: wide_ref[n, where, :], 2 * GROUP, turns_ref, turned_ref)


def weighted_corr(got_ref, params_ref, table_ref, turns_ref, wide_ref, turned_ref, back_ref, corr_time_ref, brief):
    forward_both(got_ref, wide_ref, turns_ref, turned_ref)
    for first, last in PARTS:
        corr = spectra(turned_ref, table_ref, first, last, brief)[4]
        back = precise_dot(corr.reshape((last - first) * GROUP, 2 * INNER), table_ref, 1, brief)
        back_ref[first:last] = back.reshape(last - first, GROUP, 2 * INNER)

    def store(n, where, value):
        corr_time_ref[where, n * INNER : (n + 1) * INNER] = value * np.float32(1.0 / math.sqrt(4 * LENGTH))

    inverse_outer(back_ref, GROUP, turns_ref, store)
    return corr_time_ref[...] * decay_window(params_ref)


PARTS = ((0, 4), (4, 8), (8, 12), (12, HALF))
ALONG = ((1,), (1,))
TIME_SCALE = np.float32(1.0 / math.sqrt(LENGTH))


def embed_kernel(
    got_ref, slope_ref, features_ref, params_ref, table_ref, turns_ref, share_ref, wide_ref, turned_ref, back_ref, corr_time_ref
):
    weighted = weighted_corr(
        got_ref, params_ref, table_ref, turns_ref, wide_ref, turned_ref, back_ref, corr_time_ref, True
    )
    (filter_high, filter_low), (high, low) = split(params_ref[:, :GROUP]), split(weighted)
    hidden_grad = slope_ref[...] * jnp.dot(
        jnp.concatenate([filter_high, filter_low, filter_high], axis=1),
        jnp.concatenate([high, high, low], axis=0),
        preferred_element_type=jnp.float32,
    )
    crossed = lax.dot_general(
        jnp.concatenate(split(features_ref[...]), axis=0),
        jnp.concatenate(split(hidden_grad), axis=0),
        (ALONG, ((), ())),
        preferred_element_type=jnp.float32,
    )
    embed = (crossed[:32, :GROUP] + (crossed[32:, :GROUP] + crossed[:32, GROUP:])) * TIME_SCALE
    embed = jnp.concatenate([embed[:16], embed[16:]], axis=1).astype(jnp.bfloat16)
    share_ref[...] = jnp.broadcast_to(embed[None], share_ref.shape)


def conv_kernel(got_ref, taps_ref, table_ref, turns_ref, out_ref, wide_ref, turned_ref, back_ref):
    forward_both(got_ref, wide_ref, turns_ref, turned_ref)
    for first, last in PARTS:
        in_real, in_imag, up_real, up_imag, _ = spectra(turned_ref, table_ref, first, last)
        tap_real, tap_imag = taps_ref[first:last, :, :INNER], taps_ref[first:last, :, INNER:]
        conv = pair(tap_real * in_real - tap_imag * in_imag, tap_real * in_imag + tap_imag * in_real)
        grad = pair(tap_real * up_real + tap_imag * up_imag, tap_real * up_imag - tap_imag * up_real)
        joined = jnp.concatenate([conv, grad], axis=1)
        back = precise_dot(joined.reshape((last - first) * 2 * GROUP, 2 * INNER), table_ref, 1)
        back_ref[first:last] = back.reshape(last - first, 2 * GROUP, 2 * INNER)

    def store(n, where, value):
        wide_ref[n, where, :] = value

    inverse_outer(back_ref, 2 * GROUP, turns_ref, store)
    for n in range(BLOCKS):
        out_ref[n, : 2 * GROUP] = wide_ref[n].astype(jnp.bfloat16)
        out_ref[n, 2 * GROUP :] = jnp.zeros((16, INNER), jnp.bfloat16)


def grads_kernel(
    got_ref, hidden_ref, params_ref, table_ref, turns_ref, grads_ref, wide_ref, turned_ref, back_ref, corr_time_ref
):
    weighted = weighted_corr(
        got_ref, params_ref, table_ref, turns_ref, wide_ref, turned_ref, back_ref, corr_time_ref, False
    )
    grads_ref[:, :GROUP] = precise(hidden_ref[...], weighted, ALONG) * TIME_SCALE
    slopes = weighted * precise(params_ref[:, :GROUP], hidden_ref[...], ((0,), (0,)))
    inner = lax.broadcasted_iota(jnp.int32, (1, INNER), 1)
    rate = jnp.zeros((GROUP, INNER), jnp.float32)
    for n in range(BLOCKS):
        positions = (inner + n * INNER).astype(jnp.float32) / LENGTH
        rate += positions * slopes[:, n * INNER : (n + 1) * INNER]
    grads_ref[:, GROUP:] = precise(jnp.full((GROUP, INNER), -1.0, jnp.float32), rate, ALONG) * TIME_SCALE


def insert_kernel(shares_ref, _, out_hbm, total_ref, sems):
    total_ref[...] = jnp.sum(shares_ref[...].astype(jnp.float32), axis=0).astype(jnp.bfloat16)
    copies = []
    for n in range(BLOCKS):
        target = out_hbm.at[n, pl.ds(2 * GROUP, 16)]
        copies.append(pltpu.make_async_copy(total_ref, target, sems.at[n]))
        copies[-1].start()
    for copy in copies:
        copy.wait()


def apply_kernel(got_ref, key_ref, value_ref, grad_ref, d_query_ref, d_key_ref, d_value_ref, embed_ref):
    total = jnp.sum(got_ref[:, 2 * GROUP :, :].astype(jnp.float32), axis=0)
    embed_ref[:16] = total[:, :GROUP]
    embed_ref[16:] = total[:, GROUP:]
    for pair in range(BLOCKS // 2):
        lanes = slice(2 * GROUP * pair, 2 * GROUP * (pair + 1))

        def times(place):
            both = [got_ref[2 * pair + i, place : place + GROUP].astype(jnp.float32) for i in (0, 1)]
            return jnp.concatenate(both, axis=0).T

        conv, grad = times(0), times(GROUP)
        d_query_ref[0, :, lanes] = (grad_ref[0, :, lanes].astype(jnp.float32) * conv).astype(jnp.bfloat16)
        d_key_ref[0, :, lanes] = (grad * value_ref[0, :, lanes].astype(jnp.float32)).astype(jnp.bfloat16)
        d_value_ref[0, :, lanes] = (grad * key_ref[0, :, lanes].astype(jnp.float32)).astype(jnp.bfloat16)


def call(kernel, outs, ins, scratch=(), in_specs=None, out_specs=None, aliases=(), megabytes=8):
    return pl.pallas_call(
        kernel,
        out_shape=[jax.ShapeDtypeStruct(shape, dtype) for shape, dtype in outs],
        in_specs=in_specs or [VMEM] * len(ins),
        out_specs=out_specs or [VMEM] * len(outs),
        scratch_shapes=list(scratch),
        input_output_aliases=dict(aliases),
        compiler_params=pltpu.CompilerParams(vmem_limit_bytes=megabytes * 1024 * 1024),
    )(*ins)


def swapped_sum(value, axis, step):
    size = lax.axis_size(axis)
    return value + lax.ppermute(value, axis, [(i, i ^ step) for i in range(size)])


def per_device(query_input, key_input, value_input, grad_output, w_embed, w_filter, decay_rates):
    f32, bf16 = jnp.float32, jnp.bfloat16
    forward, turns = (jnp.asarray(t) for t in tables())
    features = jnp.asarray(embed_features(w_embed.shape[0]))
    spectrum = (HALF, GROUP, 2 * INNER)
    piece = (INNER, query_input.shape[2])
    moved = (BLOCKS, 2 * GROUP, INNER)
    loaded = (BLOCKS, 2 * GROUP + 16, INNER)
    flat = (GROUP, LENGTH)
    (sent,) = call(
        pack_kernel,
        [(moved, bf16)],
        (query_input, key_input, value_input, grad_output),
        [pltpu.VMEM(piece, bf16)] * 4
        + [pltpu.VMEM(moved, bf16), pltpu.SemaphoreType.DMA((16,)), pltpu.SemaphoreType.DMA((4,))],
        in_specs=[HBM] * 4,
        out_specs=[HBM],
        megabytes=58,
    )
    got = lax.all_to_all(sent, "seq", split_axis=0, concat_axis=0, tiled=True)
    pre = jnp.einsum("ej,et->jt", w_embed, features, precision=lax.Precision.HIGHEST)
    hidden, slope = jnp.sin(pre), jnp.cos(pre)
    params = jnp.concatenate(
        [w_filter, jnp.broadcast_to(decay_rates[:, None], (GROUP, INNER - GROUP))], axis=1
    )
    (taps_spec,) = call(
        filter_kernel,
        [(spectrum, f32)],
        (hidden, params, forward, turns),
        [pltpu.VMEM(flat, f32), pltpu.VMEM(spectrum, f32)],
        megabytes=16,
    )
    plane = ("dp", "chan")
    both = (HALF, 2 * GROUP, 2 * INNER)
    got, taps_spec = lax.optimization_barrier((got, taps_spec))
    corr_scratch = [pltpu.VMEM(shape, f32) for shape in (moved, both, spectrum, flat)]
    (shares,) = call(
        embed_kernel,
        [((lax.axis_size(plane), 16, INNER), bf16)],
        (got, slope, features, params, forward, turns),
        corr_scratch,
        megabytes=24,
    )
    shares = lax.all_to_all(shares, plane, split_axis=0, concat_axis=0, tiled=True)
    (result,) = call(
        conv_kernel,
        [(loaded, bf16)],
        (got, taps_spec, forward, turns),
        [pltpu.VMEM(moved, f32), pltpu.VMEM(both, f32), pltpu.VMEM(both, f32)],
        megabytes=24,
    )
    (result,) = call(
        insert_kernel,
        [(loaded, bf16)],
        (shares, result),
        [pltpu.VMEM((16, INNER), bf16), pltpu.SemaphoreType.DMA((BLOCKS,))],
        in_specs=[VMEM, HBM],
        out_specs=[HBM],
        aliases=((1, 0),),
        megabytes=4,
    )
    result, got = lax.optimization_barrier((result, got))
    back = lax.all_to_all(result, "seq", split_axis=0, concat_axis=0, tiled=True)
    (grads,) = call(
        grads_kernel,
        [((GROUP, 2 * GROUP), f32)],
        (got, hidden, params, forward, turns),
        corr_scratch,
        megabytes=24,
    )
    grads = swapped_sum(swapped_sum(grads, "dp", 1), "dp", 2)
    d_query, d_key, d_value, grad_embed = call(
        apply_kernel,
        [(query_input.shape, bf16)] * 3 + [(w_embed.shape, f32)],
        (back, key_input, value_input, grad_output),
        megabytes=12,
    )
    return (d_query, d_key, d_value, grads[:, :GROUP], grads[0, GROUP:], grad_embed)


def solution(mesh):
    wide = P("dp", "seq", "chan")
    split = ("chan", "seq")
    return jax.shard_map(
        per_device,
        mesh=mesh,
        in_specs=(wide, wide, wide, wide, P(), P(None, split), P(split)),
        out_specs=(wide, wide, wide, P(None, split), P(split), P()),
        check_vma=False,
    )
```

```python
import math

import jax
import jax.numpy as jnp
import numpy as np
from jax import lax
from jax.experimental import pallas as pl
from jax.experimental.pallas import tpu as pltpu
from jax.sharding import PartitionSpec as P

BLOCKS = 16
INNER = 128
GROUP = 64
HALF = 17
LENGTH = BLOCKS * INNER
PERIOD = 2 * LENGTH
VMEM = pl.BlockSpec(memory_space=pltpu.VMEM)
HBM = pl.BlockSpec(memory_space=pltpu.HBM)


def split_table(table):
    high = table.astype(jnp.bfloat16)
    low = (table - high.astype(np.float64)).astype(jnp.bfloat16)
    return np.stack([high, low])


def tables():
    inner = np.arange(INNER)
    angle = 2.0 * math.pi * (np.outer(inner, inner) % INNER) / INNER
    cos, sin = np.cos(angle), np.sin(angle)
    forward = np.block([[cos, -sin], [sin, cos]])
    turn = 2.0 * math.pi * np.outer(np.arange(HALF), inner) / PERIOD
    weight = np.full((HALF, 1), 2.0 / PERIOD)
    weight[0] = weight[-1] = 1.0 / PERIOD
    turns = np.zeros((4, 24, INNER), np.float32)
    for i, part in enumerate((np.cos(turn), np.sin(turn), np.cos(turn) * weight, np.sin(turn) * weight)):
        turns[i, :HALF] = part
    return split_table(forward), turns


def embed_features(count):
    bands = np.arange(count // 2) + 0.5
    phase = np.arange(LENGTH)[None, :] * bands[:, None] * (2.0 * math.pi / LENGTH)
    return np.concatenate([np.sin(phase), np.cos(phase)], axis=0).astype(np.float32)


def weighted_sum(terms):
    total = None
    for value, factor in terms:
        if abs(factor) < 1e-9:
            continue
        if abs(factor - 1.0) < 1e-9:
            total = value if total is None else total + value
        elif abs(factor + 1.0) < 1e-9:
            total = -value if total is None else total - value
        else:
            part = value * np.float32(factor)
            total = part if total is None else total + part
    return total


def odd_bins(x):
    size = len(x)
    half = size // 2
    if size == 2:
        return {1: (x[0], -x[1])}
    minus = {n: x[n] - x[size - n] for n in range(1, half)}
    plus = {n: x[n] + x[size - n] for n in range(1, half)}
    minus[0] = x[0]
    plus[half] = x[half]
    out = {}
    for k in range(1, half, 2):
        cos = lambda n: math.cos(math.pi * k * n / size)
        sin = lambda n: math.sin(math.pi * k * n / size)
        cos_even = weighted_sum([(minus[n], cos(n)) for n in range(0, half, 2)])
        cos_odd = weighted_sum([(minus[n], cos(n)) for n in range(1, half, 2)])
        sin_even = weighted_sum([(plus[n], sin(n)) for n in range(2, half + 1, 2)])
        sin_odd = weighted_sum([(plus[n], sin(n)) for n in range(1, half, 2)])
        out[k] = (cos_even + cos_odd, -(sin_even + sin_odd))
        out[size - k] = (cos_even - cos_odd, sin_even - sin_odd)
    return out


def real_bins(x):
    size = len(x)
    half = size // 2
    if size == 2:
        return {0: (x[0] + x[1], None), 1: (x[0] - x[1], None)}
    out = {2 * k: v for k, v in real_bins([x[n] + x[n + half] for n in range(half)]).items()}
    out.update(odd_bins([x[n] - x[n + half] for n in range(half)]))
    return out


def outer_bins(x):
    out = {2 * k: v for k, v in real_bins(x).items()}
    out.update(odd_bins(x))
    return out


def odd_times(bins, size):
    half = size // 2
    if size == 2:
        return [bins[1][0], -bins[1][1]]
    ks = range(1, half, 2)
    real_plus = {k: bins[k][0] + bins[size - k][0] for k in ks}
    real_minus = {k: bins[k][0] - bins[size - k][0] for k in ks}
    imag_plus = {k: bins[k][1] + bins[size - k][1] for k in ks}
    imag_minus = {k: bins[k][1] - bins[size - k][1] for k in ks}
    out = [None] * size
    for n in range(half + 1):
        reals, imags = (real_minus, imag_plus) if n % 2 else (real_plus, imag_minus)
        cos = weighted_sum([(reals[k], math.cos(math.pi * k * n / size)) for k in ks])
        sin = weighted_sum([(imags[k], math.sin(math.pi * k * n / size)) for k in ks])
        if n == 0:
            out[0] = cos
        elif n == half:
            out[half] = -sin
        else:
            out[n] = cos - sin
            out[size - n] = -(cos + sin)
    return out


def real_times(bins, size):
    if size == 2:
        return [bins[0][0] + bins[1][0], bins[0][0] - bins[1][0]]
    half = size // 2
    even = real_times({k // 2: v for k, v in bins.items() if k % 2 == 0}, half)
    odd = odd_times({k: v for k, v in bins.items() if k % 2}, half)
    return [even[n] + odd[n] for n in range(half)] + [even[n] - odd[n] for n in range(half)]


def outer_times(bins, size):
    even = real_times({k // 2: v for k, v in bins.items() if k % 2 == 0}, size)
    odd = odd_times({k: v for k, v in bins.items() if k % 2}, size)
    return [even[n] + odd[n] for n in range(size)]


def split(values):
    high = values.astype(jnp.bfloat16)
    return high, (values - high.astype(jnp.float32)).astype(jnp.bfloat16)


def precise_dot(values, table_ref, side=0, brief=False):
    high, low = split(values)
    dims = (((1,), (side,)), ((), ()))
    dot = lambda a, b: lax.dot_general(a, b, dims, preferred_element_type=jnp.float32)
    rest = dot(high, table_ref[1])
    if not brief:
        rest = dot(low, table_ref[0]) + rest
    return dot(high, table_ref[0]) + rest


def forward_outer(load, rows, turns_ref, turned_ref):
    @pl.loop(0, rows // 8, unroll=4)
    def _(step):
        where = pl.ds(pl.multiple_of(step * 8, 8), 8)
        bins = outer_bins([load(n, where) for n in range(BLOCKS)])
        for k in range(HALF):
            real, imag = bins[k]
            cos, sin = turns_ref[0, k : k + 1, :], turns_ref[1, k : k + 1, :]
            if k == 0:
                turned_real, turned_imag = real, jnp.zeros_like(real)
            elif imag is None:
                turned_real, turned_imag = real * cos, -real * sin
            else:
                turned_real, turned_imag = real * cos + imag * sin, imag * cos - real * sin
            turned_ref[k, where, :INNER] = turned_real
            turned_ref[k, where, INNER:] = turned_imag


def inverse_outer(back_ref, rows, turns_ref, store):
    @pl.loop(0, rows // 8, unroll=4)
    def _(step):
        where = pl.ds(pl.multiple_of(step * 8, 8), 8)
        bins = {}
        for k in range(HALF):
            real, imag = back_ref[k, where, :INNER], back_ref[k, where, INNER:]
            cos, sin = turns_ref[2, k : k + 1, :], turns_ref[3, k : k + 1, :]
            if k in (0, HALF - 1):
                bins[k] = (real * cos - imag * sin, None)
            else:
                bins[k] = (real * cos - imag * sin, real * sin + imag * cos)
        for n, value in enumerate(outer_times(bins, BLOCKS)):
            store(n, where, value)


def pack_kernel(
    query_hbm, key_hbm, value_hbm, grad_hbm, sent_hbm, key_ref, value_ref, grad_ref, query_ref, sent_ref, sems, out_sems
):
    sources = (key_hbm, value_hbm, grad_hbm, query_hbm)
    targets = (key_ref, value_ref, grad_ref, query_ref)
    copies = {}
    for part in range(4):
        lanes = pl.ds(4 * GROUP * part, 4 * GROUP)
        for i in range(4):
            source, target = sources[i].at[0, :, lanes], targets[i].at[:, lanes]
            copies[part, i] = pltpu.make_async_copy(source, target, sems.at[4 * part + i])
            copies[part, i].start()
    outs = []
    for part in range(4):
        for i in range(4):
            copies[part, i].wait()
        for pair in (2 * part, 2 * part + 1):
            lanes = slice(2 * GROUP * pair, 2 * GROUP * (pair + 1))
            for place, first, second in ((0, key_ref, value_ref), (GROUP, grad_ref, query_ref)):
                both = first[:, lanes].astype(jnp.float32) * second[:, lanes].astype(jnp.float32)
                both = both.T.astype(jnp.bfloat16)
                sent_ref[2 * pair, place : place + GROUP] = both[:GROUP]
                sent_ref[2 * pair + 1, place : place + GROUP] = both[GROUP:]
        where = pl.ds(4 * part, 4)
        outs.append(pltpu.make_async_copy(sent_ref.at[where], sent_hbm.at[where], out_sems.at[part]))
        outs[-1].start()
    for copy in outs:
        copy.wait()


def decay_window(params_ref):
    positions = lax.broadcasted_iota(jnp.int32, (1, LENGTH), 1).astype(jnp.float32)
    return jnp.exp(-params_ref[:, GROUP : GROUP + 1] * positions / LENGTH)


def filter_kernel(hidden_ref, params_ref, table_ref, turns_ref, spec_ref, taps_ref, turned_ref):
    taps_ref[...] = decay_window(params_ref) * lax.dot_general(
        params_ref[:, :GROUP],
        hidden_ref[...],
        (((0,), (0,)), ((), ())),
        precision=lax.Precision.HIGHEST,
        preferred_element_type=jnp.float32,
    )
    forward_outer(
        lambda n, where: taps_ref[where, n * INNER : (n + 1) * INNER], GROUP, turns_ref, turned_ref
    )
    turned = turned_ref[...].reshape(HALF * GROUP, 2 * INNER)
    spec_ref[...] = precise_dot(turned, table_ref).reshape(HALF, GROUP, 2 * INNER)


def precise(a, b, dims):
    (a_high, a_low), (b_high, b_low) = split(a), split(b)
    dot = lambda x, y: lax.dot_general(x, y, (dims, ((), ())), preferred_element_type=jnp.float32)
    return dot(a_high, b_high) + (dot(a_low, b_high) + dot(a_high, b_low))


def spectra(turned_ref, table_ref, first, last, brief=False):
    count = last - first
    turned = turned_ref[first:last].reshape(count * 2 * GROUP, 2 * INNER)
    spec = precise_dot(turned, table_ref, brief=brief).reshape(count, 2 * GROUP, 2 * INNER)
    in_real, in_imag = spec[:, :GROUP, :INNER], spec[:, :GROUP, INNER:]
    up_real, up_imag = spec[:, GROUP:, :INNER], spec[:, GROUP:, INNER:]
    corr = pair(in_real * up_real + in_imag * up_imag, in_real * up_imag - in_imag * up_real)
    return in_real, in_imag, up_real, up_imag, corr


def pair(real, imag):
    return jnp.concatenate([real, imag], axis=2)


def forward_both(got_ref, wide_ref, turns_ref, turned_ref):
    wide_ref[...] = got_ref[...].astype(jnp.float32)
    forward_outer(lambda n, where: wide_ref[n, where, :], 2 * GROUP, turns_ref, turned_ref)


def weighted_corr(got_ref, params_ref, table_ref, turns_ref, wide_ref, turned_ref, back_ref, corr_time_ref, brief):
    forward_both(got_ref, wide_ref, turns_ref, turned_ref)
    for first, last in PARTS:
        corr = spectra(turned_ref, table_ref, first, last, brief)[4]
        back = precise_dot(corr.reshape((last - first) * GROUP, 2 * INNER), table_ref, 1, brief)
        back_ref[first:last] = back.reshape(last - first, GROUP, 2 * INNER)

    def store(n, where, value):
        corr_time_ref[where, n * INNER : (n + 1) * INNER] = value * np.float32(1.0 / math.sqrt(4 * LENGTH))

    inverse_outer(back_ref, GROUP, turns_ref, store)
    return corr_time_ref[...] * decay_window(params_ref)


PARTS = ((0, 4), (4, 8), (8, 12), (12, HALF))
ALONG = ((1,), (1,))
TIME_SCALE = np.float32(1.0 / math.sqrt(LENGTH))


def embed_kernel(
    got_ref, slope_ref, features_ref, params_ref, table_ref, turns_ref, share_ref, wide_ref, turned_ref, back_ref, corr_time_ref
):
    weighted = weighted_corr(
        got_ref, params_ref, table_ref, turns_ref, wide_ref, turned_ref, back_ref, corr_time_ref, True
    )
    (filter_high, filter_low), (high, low) = split(params_ref[:, :GROUP]), split(weighted)
    hidden_grad = slope_ref[...] * jnp.dot(
        jnp.concatenate([filter_high, filter_low, filter_high], axis=1),
        jnp.concatenate([high, high, low], axis=0),
        preferred_element_type=jnp.float32,
    )
    crossed = lax.dot_general(
        jnp.concatenate(split(features_ref[...]), axis=0),
        jnp.concatenate(split(hidden_grad), axis=0),
        (ALONG, ((), ())),
        preferred_element_type=jnp.float32,
    )
    embed = (crossed[:32, :GROUP] + (crossed[32:, :GROUP] + crossed[:32, GROUP:])) * TIME_SCALE
    embed = jnp.concatenate([embed[:16], embed[16:]], axis=1).astype(jnp.bfloat16)
    share_ref[...] = jnp.broadcast_to(embed[None], share_ref.shape)


def conv_kernel(got_ref, taps_ref, table_ref, turns_ref, out_ref, wide_ref, turned_ref, back_ref):
    forward_both(got_ref, wide_ref, turns_ref, turned_ref)
    for first, last in PARTS:
        in_real, in_imag, up_real, up_imag, _ = spectra(turned_ref, table_ref, first, last)
        tap_real, tap_imag = taps_ref[first:last, :, :INNER], taps_ref[first:last, :, INNER:]
        conv = pair(tap_real * in_real - tap_imag * in_imag, tap_real * in_imag + tap_imag * in_real)
        grad = pair(tap_real * up_real + tap_imag * up_imag, tap_real * up_imag - tap_imag * up_real)
        joined = jnp.concatenate([conv, grad], axis=1)
        back = precise_dot(joined.reshape((last - first) * 2 * GROUP, 2 * INNER), table_ref, 1)
        back_ref[first:last] = back.reshape(last - first, 2 * GROUP, 2 * INNER)

    def store(n, where, value):
        wide_ref[n, where, :] = value

    inverse_outer(back_ref, 2 * GROUP, turns_ref, store)
    for n in range(BLOCKS):
        out_ref[n, : 2 * GROUP] = wide_ref[n].astype(jnp.bfloat16)
        out_ref[n, 2 * GROUP :] = jnp.zeros((16, INNER), jnp.bfloat16)


def grads_kernel(
    got_ref, hidden_ref, params_ref, table_ref, turns_ref, grads_ref, wide_ref, turned_ref, back_ref, corr_time_ref
):
    weighted = weighted_corr(
        got_ref, params_ref, table_ref, turns_ref, wide_ref, turned_ref, back_ref, corr_time_ref, False
    )
    grads_ref[:, :GROUP] = precise(hidden_ref[...], weighted, ALONG) * TIME_SCALE
    slopes = weighted * precise(params_ref[:, :GROUP], hidden_ref[...], ((0,), (0,)))
    inner = lax.broadcasted_iota(jnp.int32, (1, INNER), 1)
    rate = jnp.zeros((GROUP, INNER), jnp.float32)
    for n in range(BLOCKS):
        positions = (inner + n * INNER).astype(jnp.float32) / LENGTH
        rate += positions * slopes[:, n * INNER : (n + 1) * INNER]
    grads_ref[:, GROUP:] = precise(jnp.full((GROUP, INNER), -1.0, jnp.float32), rate, ALONG) * TIME_SCALE


def insert_kernel(shares_ref, _, out_hbm, total_ref, sems):
    total_ref[...] = jnp.sum(shares_ref[...].astype(jnp.float32), axis=0).astype(jnp.bfloat16)
    copies = []
    for n in range(BLOCKS):
        target = out_hbm.at[n, pl.ds(2 * GROUP, 16)]
        copies.append(pltpu.make_async_copy(total_ref, target, sems.at[n]))
        copies[-1].start()
    for copy in copies:
        copy.wait()


def apply_kernel(got_ref, key_ref, value_ref, grad_ref, d_query_ref, d_key_ref, d_value_ref, embed_ref):
    total = jnp.sum(got_ref[:, 2 * GROUP :, :].astype(jnp.float32), axis=0)
    embed_ref[:16] = total[:, :GROUP]
    embed_ref[16:] = total[:, GROUP:]
    for pair in range(BLOCKS // 2):
        lanes = slice(2 * GROUP * pair, 2 * GROUP * (pair + 1))

        def times(place):
            both = [got_ref[2 * pair + i, place : place + GROUP].astype(jnp.float32) for i in (0, 1)]
            return jnp.concatenate(both, axis=0).T

        conv, grad = times(0), times(GROUP)
        d_query_ref[0, :, lanes] = (grad_ref[0, :, lanes].astype(jnp.float32) * conv).astype(jnp.bfloat16)
        d_key_ref[0, :, lanes] = (grad * value_ref[0, :, lanes].astype(jnp.float32)).astype(jnp.bfloat16)
        d_value_ref[0, :, lanes] = (grad * key_ref[0, :, lanes].astype(jnp.float32)).astype(jnp.bfloat16)


def call(kernel, outs, ins, scratch=(), in_specs=None, out_specs=None, aliases=(), megabytes=8):
    return pl.pallas_call(
        kernel,
        out_shape=[jax.ShapeDtypeStruct(shape, dtype) for shape, dtype in outs],
        in_specs=in_specs or [VMEM] * len(ins),
        out_specs=out_specs or [VMEM] * len(outs),
        scratch_shapes=list(scratch),
        input_output_aliases=dict(aliases),
        compiler_params=pltpu.CompilerParams(vmem_limit_bytes=megabytes * 1024 * 1024),
    )(*ins)


def swapped_sum(value, axis, step):
    size = lax.axis_size(axis)
    return value + lax.ppermute(value, axis, [(i, i ^ step) for i in range(size)])


def per_device(query_input, key_input, value_input, grad_output, w_embed, w_filter, decay_rates):
    f32, bf16 = jnp.float32, jnp.bfloat16
    forward, turns = (jnp.asarray(t) for t in tables())
    features = jnp.asarray(embed_features(w_embed.shape[0]))
    spectrum = (HALF, GROUP, 2 * INNER)
    piece = (INNER, query_input.shape[2])
    moved = (BLOCKS, 2 * GROUP, INNER)
    loaded = (BLOCKS, 2 * GROUP + 16, INNER)
    flat = (GROUP, LENGTH)
    (sent,) = call(
        pack_kernel,
        [(moved, bf16)],
        (query_input, key_input, value_input, grad_output),
        [pltpu.VMEM(piece, bf16)] * 4
        + [pltpu.VMEM(moved, bf16), pltpu.SemaphoreType.DMA((16,)), pltpu.SemaphoreType.DMA((4,))],
        in_specs=[HBM] * 4,
        out_specs=[HBM],
        megabytes=58,
    )
    got = lax.all_to_all(sent, "seq", split_axis=0, concat_axis=0, tiled=True)
    pre = jnp.einsum("ej,et->jt", w_embed, features, precision=lax.Precision.HIGHEST)
    hidden, slope = jnp.sin(pre), jnp.cos(pre)
    params = jnp.concatenate(
        [w_filter, jnp.broadcast_to(decay_rates[:, None], (GROUP, INNER - GROUP))], axis=1
    )
    (taps_spec,) = call(
        filter_kernel,
        [(spectrum, f32)],
        (hidden, params, forward, turns),
        [pltpu.VMEM(flat, f32), pltpu.VMEM(spectrum, f32)],
        megabytes=16,
    )
    plane = ("dp", "chan")
    both = (HALF, 2 * GROUP, 2 * INNER)
    got, taps_spec = lax.optimization_barrier((got, taps_spec))
    corr_scratch = [pltpu.VMEM(shape, f32) for shape in (moved, both, spectrum, flat)]
    (shares,) = call(
        embed_kernel,
        [((lax.axis_size(plane), 16, INNER), bf16)],
        (got, slope, features, params, forward, turns),
        corr_scratch,
        megabytes=24,
    )
    shares = lax.all_to_all(shares, plane, split_axis=0, concat_axis=0, tiled=True)
    (result,) = call(
        conv_kernel,
        [(loaded, bf16)],
        (got, taps_spec, forward, turns),
        [pltpu.VMEM(moved, f32), pltpu.VMEM(both, f32), pltpu.VMEM(both, f32)],
        megabytes=24,
    )
    (result,) = call(
        insert_kernel,
        [(loaded, bf16)],
        (shares, result),
        [pltpu.VMEM((16, INNER), bf16), pltpu.SemaphoreType.DMA((BLOCKS,))],
        in_specs=[VMEM, HBM],
        out_specs=[HBM],
        aliases=((1, 0),),
        megabytes=4,
    )
    result, got = lax.optimization_barrier((result, got))
    back = lax.all_to_all(result, "seq", split_axis=0, concat_axis=0, tiled=True)
    (grads,) = call(
        grads_kernel,
        [((GROUP, 2 * GROUP), f32)],
        (got, hidden, params, forward, turns),
        corr_scratch,
        megabytes=24,
    )
    grads = swapped_sum(swapped_sum(grads, "dp", 1), "dp", 2)
    d_query, d_key, d_value, grad_embed = call(
        apply_kernel,
        [(query_input.shape, bf16)] * 3 + [(w_embed.shape, f32)],
        (back, key_input, value_input, grad_output),
        megabytes=12,
    )
    return (d_query, d_key, d_value, grads[:, :GROUP], grads[0, GROUP:], grad_embed)


def solution(mesh):
    wide = P("dp", "seq", "chan")
    split = ("chan", "seq")
    return jax.shard_map(
        per_device,
        mesh=mesh,
        in_specs=(wide, wide, wide, wide, P(), P(None, split), P(split)),
        out_specs=(wide, wide, wide, P(None, split), P(split), P()),
        check_vma=False,
    )
```
